256 devices in a mesh: aux: 8 (over z_lo, y), virt: 32 (over x, z_hi, core).
Axes of the slice: x: 4, y: 4, z: 8 (z_hi: 4, z_lo: 2; z = z_hi * 2 + z_lo), core: 2. Of those that a mesh axis runs over, the one named last changes fastest.
Arguments:
- df_blocks: bfloat16 [512, 1280, 1280], P('aux', 'virt'), may hold values from -1.25 to 1.25
- fno_rotation: bfloat16 [1280, 640], replicated, may hold values from -0.15625 to 0.15625
- tile_pairs: int32 [64, 2], P('virt'), may hold values from 0 to 639
Outputs:
- slab_tiles: float32 [640, 64, 640], P('aux', 'virt')
The draws below stay inside these ranges and needn't reach their ends.
All inputs are finite; a program needn't handle non-finite values.
Results may differ from the reference program's by a relative error of at most 0.0057.
Values may be sent and summed in bfloat16 or wider, within the bound.
A program may use at most 64 MiB of HBM per device.

```python
import jax
import jax.numpy as jnp
from jax import lax

NV = 1280
NF = 640
NAUX = 512
NTILES = 64


def set_ends(values, stream_key, smallest, high):
    shape = values.shape
    spot = [jax.random.randint(jax.random.fold_in(stream_key, axis), (), 0, shape[axis]) for axis in range(len(shape))]
    values = values.at[tuple(spot)].set(smallest)
    longest = shape.index(max(shape))
    spot[longest] = (spot[longest] + 1) % shape[longest]
    return values.at[tuple(spot)].set(high)


def shard_levels(key, shape, shards, low, largest):
    factor_of = 1.0
    for axis_at, blocks in shards:
        steps = jax.random.uniform(jax.random.fold_in(jax.random.fold_in(key, 6), axis_at), (blocks,), jnp.float32, low / len(shards), largest / len(shards))
        factor_of = factor_of * jnp.repeat(jnp.exp(steps), shape[axis_at] // blocks).reshape((-1,) + (1,) * (len(shape) - 1 - axis_at))
    return factor_of


def gaussian(stream_key, extent, scale, reach, split=(), dtype=jnp.bfloat16):
    array = scale * jax.random.normal(stream_key, extent, jnp.float32)
    if split:
        array = array * shard_levels(stream_key, extent, split, -0.22, 0.18)
    return jnp.clip(array, -reach, reach).astype(dtype)


def setup_inputs(seed: int = 0) -> dict:
    key_of = jax.random.split(jax.random.key(seed), 4)
    return {
        "df_blocks": gaussian(key_of[0], (NAUX, NV, NV), (1.0 / NAUX ** 0.25), 1.25, ((0, 8), (1, 32))),
        "fno_rotation": gaussian(key_of[1], (NV, NF), NV ** -0.5, 0.15625),
        "tile_pairs": set_ends(jax.random.randint(key_of[2], (NTILES, 2), 0, NF), jax.random.fold_in(key_of[2], 1), 0, NF - 1).astype(jnp.int32),
    }


def reference(df_blocks, fno_rotation, tile_pairs):
    def transform_one(slice_ints):
        halfway = jnp.dot(slice_ints, fno_rotation, preferred_element_type=jnp.float32).astype(jnp.bfloat16)
        return jnp.dot(fno_rotation.T, halfway, preferred_element_type=jnp.float32).astype(jnp.bfloat16)

    fno_ints = lax.map(transform_one, df_blocks)
    left_rows = jnp.take(fno_ints, tile_pairs[:, 0], axis=1).astype(jnp.float32)
    right_rows = jnp.take(fno_ints, tile_pairs[:, 1], axis=1).astype(jnp.float32)
    return jnp.einsum('ptc,ptd->ctd', left_rows, right_rows)
```

```python
import functools

import jax
import jax.numpy as jnp
import numpy as np
from jax import lax
from jax.experimental import pallas as pl
from jax.experimental.pallas import tpu as pltpu
from jax.sharding import PartitionSpec as P

MESH = pl.DeviceIdType.MESH
BF = jnp.bfloat16
F32 = jnp.float32

ROUNDS = 4
SUB = 2
GROUPS = 4


def dot(a, b):
    return jnp.dot(a, b, preferred_element_type=F32)


def dot_nt(a, b):
    return lax.dot_general(a, b, (((1,), (1,)), ((), ())), preferred_element_type=F32)


def kernel(
    df_ref, rot_ref, pairs_ref, spread_ref, mask_ref, out_ref,
    df_v, rot_v, half_v, quad_v, pair_v, hot_v, w_v, tsend_v, town_v, trecv_v,
    zsend_v, zown_v, zrecv_v, fno_v, gsend_v, gath_v, pick_v, acc_v,
    df_sem, rot_sem, p_ssem, p_rsem, h_ssem, h_rsem, t_ssem, t_rsem,
    z_ssem, z_rsem, g_ssem, g_rsem, y_ssem, y_rsem,
):
    natural = rot_v.shape[1]
    aux = lax.axis_index("aux")
    virt = lax.axis_index("virt")
    zl, y = aux // 4, aux % 4
    x, zh, c = virt // 8, (virt // 2) % 4, virt % 2
    hrows = half_v.shape[1] // 8
    rrows = half_v.shape[1]

    def dev(zl_, y_, x_, zh_, c_):
        return (zl_ * 4 + y_, (x_ * 4 + zh_) * 2 + c_)

    def remote(src, dst, ssem, rsem, device):
        return pltpu.make_async_remote_copy(
            src_ref=src, dst_ref=dst, send_sem=ssem, recv_sem=rsem, device_id=device, device_id_type=MESH
        )

    def df_copy(i):
        return pltpu.make_async_copy(df_ref.at[pl.ds(i * rrows, rrows)], df_v.at[i], df_sem.at[i])

    rot_copy = pltpu.make_async_copy(rot_ref, rot_v, rot_sem)
    rot_copy.start()
    for i in range(ROUNDS):
        df_copy(i).start()

    xr, xl = (x + 1) % 4, (x + 3) % 4
    peers = [dev(zl, y, x, zh, 1 - c)]
    peers += [dev(zl, y, xx, zh, cc) for xx in (xr, xl) for cc in range(2)]
    peers += [dev(zl, y, x, (zh + d) % 4, c) for d in range(1, 4)]
    peers += [dev(1 - zl, y, xx, zh, cc) for xx in (x, xr, xl) for cc in range(2)]
    peers += [dev(zl, (y + d) % 4, x, zh, c) for d in range(1, 4)]
    barrier = pltpu.get_barrier_semaphore()
    for peer in peers:
        pl.semaphore_signal(barrier, inc=1, device_id=peer, device_id_type=MESH)

    row = lax.broadcasted_iota(jnp.int32, (8, 128), 0)
    tile = row % 2
    side = row // 4
    mine = jnp.where(
        side == 0,
        jnp.where(tile == 0, pairs_ref[0, 0], pairs_ref[1, 0]),
        jnp.where(tile == 0, pairs_ref[0, 1], pairs_ref[1, 1]),
    )
    pair_v[x, c, zh] = mine

    def place(col):
        u = (x + 4 - col) % 4
        j, xh = u % 2, u // 2
        return u, j, xh, (j + xh) % 2

    def quad_dst(col, q):
        u, j, xh, pq = place(col)
        jd = (q // 2 + xh) % 2
        return (xh * 2 + jd + col) % 4, q % 2

    def h_copy(i, col, d):
        u, j, xh, pq = place(col)
        q = (pq * 2 + c + d) % 4
        xd, cd = quad_dst(col, q)
        src = half_v.at[i, pl.ds(pl.multiple_of(col * 4 * hrows + q * hrows, 16), hrows)]
        dst = quad_v.at[i, col, pl.ds(pl.multiple_of((j * 2 + c) * hrows, 16), hrows)]
        if d == 0:
            return pltpu.make_async_copy(src, dst, h_rsem.at[i, col, 0])
        return remote(src, dst, h_ssem.at[i, col, d], h_rsem.at[i, col, d], dev(zl, y, xd, zh, cd))

    def half_step(i):
        df_copy(i).wait()
        half_v[i] = dot(df_v[i], rot_v[...]).astype(BF)

    def half_send(i):
        for d in (2, 3, 1, 0):
            for col in range(2):
                h_copy(i, col, d).start()

    def p_first(d):
        ref = pair_v.at[x, c, zh]
        return remote(ref, ref, p_ssem.at[d], p_rsem.at[d], dev(zl, y, x, (zh + d) % 4, c))

    def p_second(n):
        ref = pair_v.at[x, c]
        xx = (x, xr, xr, xl, xl)[n]
        cc = (1 - c, c, 1 - c, c, 1 - c)[n]
        return remote(ref, ref, p_ssem.at[4 + n], p_rsem.at[4 + n], dev(zl, y, xx, zh, cc))

    def p_third():
        ref = pair_v.at[xr]
        return remote(ref, ref, p_ssem.at[9], p_rsem.at[9], dev(zl, y, xl, zh, c))

    rot_copy.wait()
    half_step(0)
    pl.semaphore_wait(barrier, len(peers))
    half_send(0)
    for d in range(1, 4):
        p_first(d).start()
    half_step(1)
    half_send(1)
    for d in range(1, 4):
        p_first(d).wait_recv()
    for n in range(5):
        p_second(n).start()
    for n in range(5):
        p_second(n).wait_recv()
    p_third().start()

    lane = lax.broadcasted_iota(jnp.int32, (natural, 128), 1)
    col_at = lax.broadcasted_iota(jnp.int32, (natural, 128), 0)
    del lane, col_at
    pick_row = lax.broadcasted_iota(jnp.int32, (128, natural), 0)
    pick_col = lax.broadcasted_iota(jnp.int32, (128, natural), 1)
    pick_v[...] = jnp.where((pick_col == pick_row + aux * 80) & (pick_row < 80), 1.0, 0.0).astype(BF)
    acc_v[...] = jnp.zeros_like(acc_v)

    p_third().wait_recv()
    for col in range(2):
        u, j, xh, pq = place(col)
        wanted = jnp.concatenate(
            [pair_v[(2 * h + jj + col) % 4, cc, z] for h in range(2) for z in range(4) for jj in range(2) for cc in range(2)],
            axis=0,
        )
        at = lax.broadcasted_iota(jnp.int32, wanted.shape, 1)
        for n in range(natural // 128):
            hot_v[:, n * 128 : (n + 1) * 128] = jnp.where(wanted == at + n * 128, 1.0, 0.0).astype(BF)
        total = None
        for jj in range(2):
            xs = (xh * 2 + jj + col) % 4
            rows = rot_v[pl.ds(pl.multiple_of((xs * 4 + zh) * 80, 16), 80)]
            sel = dot_nt(hot_v[...], rows).astype(BF)
            part = dot(sel, spread_ref[jj])
            total = part if total is None else total + part
        w_v[col] = (total * mask_ref[...]).astype(BF)

    def t_copy(i, col):
        u, j, xh, pq = place(col)
        xd = jnp.where(j == 1, xr, xl)
        return remote(tsend_v.at[i, col], trecv_v.at[i, col], t_ssem.at[i, col], t_rsem.at[i, col], dev(zl, y, xd, zh, c))

    def t_step(i, col):
        u, j, xh, pq = place(col)
        for d in range(4):
            if d == 0:
                h_copy(i, col, 0).wait()
            else:
                h_copy(i, col, d).wait_recv()
        other = pl.ds(pl.multiple_of((1 - xh) * 128, 128), 128)
        own = pl.ds(pl.multiple_of(xh * 128, 128), 128)
        tsend_v[i, col] = dot(w_v[col, other], quad_v[i, col]).astype(BF)
        t_copy(i, col).start()
        town_v[i, col] = dot(w_v[col, own], quad_v[i, col])

    def z_copy(i, col, d):
        return remote(
            zsend_v.at[i, col, d - 1], zrecv_v.at[i, col, d - 1],
            z_ssem.at[i, col, d - 1], z_rsem.at[i, col, d - 1], dev(zl, y, x, (zh + d) % 4, c),
        )

    def z_step(i, col):
        t_copy(i, col).wait_recv()
        for d in (2, 1, 3, 0):
            rows = pl.ds(pl.multiple_of((zh + d) % 4 * 32, 32), 32)
            value = town_v[i, col, rows] + trecv_v[i, col, rows].astype(F32)
            if d:
                zsend_v[i, col, d - 1] = value.astype(BF)
                z_copy(i, col, d).start()
            else:
                zown_v[i, col] = value

    def g_copy(col, m, d):
        u, j, xh, pq = place(col)
        slot = (zl * 2 + j) * 2 + c
        to = (slot + d) % 8
        zd, jd, cd = to // 4, (to // 2) % 2, to % 2
        g = col * 2 + m
        src = gsend_v.at[g, pl.ds(pl.multiple_of((jd * 2 + cd) * 16, 16), 16)]
        dst = gath_v.at[g, y, pl.ds(pl.multiple_of(slot * 16, 16), 16)]
        if d == 0:
            return pltpu.make_async_copy(src, dst, g_rsem.at[g, 0])
        return remote(src, dst, g_ssem.at[g, d], g_rsem.at[g, d], dev(zd, y, (xh * 2 + jd + col) % 4, zh, cd))

    def f_step(i, col):
        for d in range(1, 4):
            z_copy(i, col, d).wait_recv()
        value = zown_v[i, col] + (zrecv_v[i, col, 0].astype(F32) + zrecv_v[i, col, 1].astype(F32)) + zrecv_v[
            i, col, 2
        ].astype(F32)
        fno_v[col * 2 + i // 2, :, i % 2] = value.reshape(4, 8, natural)

    def g_step(m, col):
        g = col * 2 + m
        gsend_v[g] = fno_v[g].reshape(64, natural).astype(BF)
        for d in range(8):
            g_copy(col, m, d).start()

    def y_copy(g, d):
        ref = gath_v.at[g, y]
        return remote(ref, ref, y_ssem.at[g, d - 1], y_rsem.at[g, d - 1], dev(zl, (y + d) % 4, x, zh, c))

    def y_step(m, col):
        g = col * 2 + m
        g_copy(col, m, 0).wait()
        for d in range(1, 8):
            g_copy(col, m, d).wait_recv()
        for d in (2, 1, 3):
            y_copy(g, d).start()

    def out_step(m, col):
        g = col * 2 + m
        for d in range(1, 4):
            y_copy(g, d).wait_recv()
        rows = gath_v[g].reshape(512, natural)
        left = pltpu.roll(dot_nt(pick_v[...], rows), 4, 1)
        at = lax.broadcasted_iota(jnp.int32, left.shape, 1)
        for t in range(2):
            here = (at % 8 >= 4) & (at % 2 == t)
            acc_v[t] += dot(jnp.where(here, left, 0.0).astype(BF), rows)

    def body(it, carry):
        @pl.when(it < ROUNDS)
        def _():
            for col in range(2):
                t_step(it, col)

        @pl.when(it + 2 < ROUNDS)
        def _():
            half_step(it + 2)
            half_send(it + 2)

        @pl.when((it >= 1) & (it < ROUNDS + 1))
        def _():
            for col in range(2):
                z_step(it - 1, col)

        @pl.when((it >= 2) & (it < ROUNDS + 2))
        def _():
            for col in range(2):
                f_step(it - 2, col)

        @pl.when((it == 3) | (it == 5))
        def _():
            for col in range(2):
                g_step((it - 3) // 2, col)

        @pl.when((it == 4) | (it == 6))
        def _():
            for col in range(2):
                y_step((it - 4) // 2, col)

        @pl.when((it == 5) | (it == 7))
        def _():
            for col in range(2):
                out_step((it - 5) // 2, col)

        return carry

    lax.fori_loop(0, 8, body, 0)
    out_ref[...] = acc_v[:, :80]

    for d in range(1, 4):
        p_first(d).wait_send()
    for n in range(5):
        p_second(n).wait_send()
    p_third().wait_send()

    def drain(i, carry):
        for col in range(2):
            for d in range(1, 4):
                h_copy(i, col, d).wait_send()
                z_copy(i, col, d).wait_send()
            t_copy(i, col).wait_send()
        return carry

    lax.fori_loop(0, ROUNDS, drain, 0)

    def drain_groups(m, carry):
        for col in range(2):
            for d in range(1, 8):
                g_copy(col, m, d).wait_send()
            for d in range(1, 4):
                y_copy(col * 2 + m, d).wait_send()
        return carry

    lax.fori_loop(0, 2, drain_groups, 0)


def constants():
    k = np.arange(4 * SUB * 40)
    dev, fun, orb = k // (SUB * 40), (k // 40) % SUB, k % 40
    a = np.arange(80)
    spread = np.stack(
        [(dev[None] == 2 * jj + a[:, None] // 40) & (orb[None] == a[:, None] % 40) for jj in range(2)]
    )
    r = np.arange(256)
    mask = ((r[:, None] // 2) % SUB) == fun[None]
    return spread.astype(np.float32), mask.astype(np.float32)


def solution(mesh):
    spread, mask = constants()

    def local(df_blocks, fno_rotation, tile_pairs):
        aux_n, orbs, nv = df_blocks.shape
        nf = fno_rotation.shape[1]
        rows = aux_n * orbs // ROUNDS
        vm = pltpu.VMEM
        dma = pltpu.SemaphoreType.DMA
        out = pl.pallas_call(
            kernel,
            name="tiles",
            out_shape=jax.ShapeDtypeStruct((2, 80, nf), F32),
            in_specs=[
                pl.BlockSpec(memory_space=pl.ANY),
                pl.BlockSpec(memory_space=pl.ANY),
                pl.BlockSpec(memory_space=pltpu.SMEM),
                pl.BlockSpec(memory_space=pltpu.VMEM),
                pl.BlockSpec(memory_space=pltpu.VMEM),
            ],
            out_specs=pl.BlockSpec(memory_space=pltpu.VMEM),
            scratch_shapes=[
                vm((ROUNDS, rows, nv), BF),
                vm((nv, nf), BF),
                vm((ROUNDS, rows, nf), BF),
                vm((ROUNDS, 2, rows // 2, nf), BF),
                vm((4, 2, 4, 8, 128), jnp.int32),
                vm((256, nf), BF),
                vm((2, 256, 4 * SUB * 40), BF),
                vm((ROUNDS, 2, 128, nf), BF),
                vm((ROUNDS, 2, 128, nf), F32),
                vm((ROUNDS, 2, 128, nf), BF),
                vm((ROUNDS, 2, 3, 32, nf), BF),
                vm((ROUNDS, 2, 32, nf), F32),
                vm((ROUNDS, 2, 3, 32, nf), BF),
                vm((GROUPS, 4, 2, 8, nf), F32),
                vm((GROUPS, 64, nf), BF),
                vm((GROUPS, 4, 128, nf), BF),
                vm((128, nf), BF),
                vm((2, 128, nf), F32),
                dma((ROUNDS,)),
                dma(()),
                dma((10,)), dma((10,)),
                dma((ROUNDS, 2, 4)), dma((ROUNDS, 2, 4)),
                dma((ROUNDS, 2)), dma((ROUNDS, 2)),
                dma((ROUNDS, 2, 3)), dma((ROUNDS, 2, 3)),
                dma((GROUPS, 8)), dma((GROUPS, 8)),
                dma((GROUPS, 3)), dma((GROUPS, 3)),
            ],
            compiler_params=pltpu.CompilerParams(
                collective_id=0, has_side_effects=True, vmem_limit_bytes=58 * 2**20
            ),
        )(
            df_blocks.reshape(aux_n * orbs, nv),
            fno_rotation,
            tile_pairs,
            jnp.asarray(spread, BF),
            jnp.asarray(mask, F32),
        )
        return jnp.transpose(out, (1, 0, 2))

    placed = (P("aux", "virt", None), P(), P("virt", None))
    return jax.shard_map(local, mesh=mesh, in_specs=placed, out_specs=P("aux", "virt", None), check_vma=False)
```

```python
import jax
import jax.numpy as jnp
import numpy as np
from jax import lax
from jax.experimental import pallas as pl
from jax.experimental.pallas import tpu as pltpu
from jax.sharding import PartitionSpec as P

MESH = pl.DeviceIdType.MESH
BF = jnp.bfloat16
F32 = jnp.float32

ROUNDS = 4
Z_FIRST = ()
FIRST, SECOND = (2, 1, 0), (3,)
LATE = ()
SPLIT = (3,)
PLAN = (
    "t0", "h2", "t1", "h3", "a0", "b0", "t2", "a1", "f0", "b1", "t3", "a2", "f1", "y0", "a3", "b2", "b3",
    "y1", "f2", "f3", "o0", "y2", "y3", "o1", "o2", "d0", "o3",
)
SUB = 2


def pieces(i):
    return ((0, 384), (384, 256)) if i in SPLIT else ((0, 640),)


def dot(a, b):
    return jnp.dot(a, b, preferred_element_type=F32)


def dot_nt(a, b):
    return lax.dot_general(a, b, (((1,), (1,)), ((), ())), preferred_element_type=F32)


def kernel(
    df_ref, rot_ref, pairs_ref, spread_ref, mask_ref, out_ref,
    spread_v, mask_v, df_v, rot_v, half_v, quad_v, pair_v, pack_v, hot_v, w_v, tsend_v, town_v, trecv_v,
    asend_v, aown_v, arecv_v, bsend_v, bown_v, brecv_v, gsend_v, gath_v, order_v, pick_v, rows_v, ysend_v, acc_v,
    c_sem, df_sem, rot_sem, p_ssem, p_rsem, h_ssem, h_rsem, t_ssem, t_rsem,
    a_ssem, a_rsem, b_ssem, b_rsem, g_ssem, g_rsem, y_ssem, y_rsem, o_sem,
):
    natural = rot_v.shape[1]
    aux = lax.axis_index("aux")
    virt = lax.axis_index("virt")
    zl, y = aux // 4, aux % 4
    x, zh, c = virt // 8, (virt // 2) % 4, virt % 2
    hrows = half_v.shape[1] // 8
    rrows = half_v.shape[1]

    def dev(zl_, y_, x_, zh_, c_):
        return (zl_ * 4 + y_, (x_ * 4 + zh_) * 2 + c_)

    def remote(src, dst, ssem, rsem, device):
        return pltpu.make_async_remote_copy(
            src_ref=src, dst_ref=dst, send_sem=ssem, recv_sem=rsem, device_id=device, device_id_type=MESH
        )

    def landed(ref, sem):
        pltpu.make_async_copy(ref, ref, sem).wait()

    def df_copy(i):
        return pltpu.make_async_copy(df_ref.at[pl.ds(i * rrows, rrows)], df_v.at[i], df_sem.at[i])

    rot_copy = pltpu.make_async_copy(rot_ref, rot_v, rot_sem)
    rot_copy.start()
    df_copy(0).start()

    xr, xl = (x + 1) % 4, (x + 3) % 4
    xo = (x + 2) % 4
    peers = [dev(zl, y, x, zh, 1 - c)]
    peers += [dev(zl, y, xx, zh, cc) for xx in (xr, xl, xo) for cc in range(2)]
    peers += [dev(zl, y, x, (zh + d) % 4, c) for d in range(1, 4)]
    peers += [dev(1 - zl, y, xx, zh, cc) for xx in (x, xr, xl) for cc in range(2)]
    peers += [dev(zl, (y + d) % 4, x, zh, c) for d in range(1, 4)]
    barrier = pltpu.get_barrier_semaphore()
    for peer in peers:
        pl.semaphore_signal(barrier, inc=1, device_id=peer, device_id_type=MESH)

    row = lax.broadcasted_iota(jnp.int32, (8, 128), 0)
    tile = row % 2
    side = row // 4
    mine = jnp.where(
        side == 0,
        jnp.where(tile == 0, pairs_ref[0, 0], pairs_ref[1, 0]),
        jnp.where(tile == 0, pairs_ref[0, 1], pairs_ref[1, 1]),
    )
    pair_v[zh, x * 2 + c] = mine

    def place(col):
        u = (x + 4 - col) % 4
        j, xh = u % 2, u // 2
        return u, j, xh, (j + xh) % 2

    def quad_dst(col, q):
        u, j, xh, pq = place(col)
        jd = (q // 2 + xh) % 2
        return (xh * 2 + jd + col) % 4, q % 2

    def h_copy(i, col, d):
        u, j, xh, pq = place(col)
        q = (pq + d // 2) % 2 * 2 + (c + d % 2) % 2
        xd, cd = quad_dst(col, q)
        src = half_v.at[i, pl.ds(pl.multiple_of(col * 4 * hrows + q * hrows, 16), hrows)]
        dst = quad_v.at[i, col, pl.ds(pl.multiple_of((j * 2 + c) * hrows, 16), hrows)]
        if d == 0:
            return pltpu.make_async_copy(src, dst, h_rsem.at[i, col])
        return remote(src, dst, h_ssem, h_rsem.at[i, col], dev(zl, y, xd, zh, cd))

    def half_step(i):
        df_copy(i).wait()
        half_v[i] = dot(df_v[i], rot_v[...]).astype(BF)

    def half_send(i, ds=(2, 3, 1, 0)):
        for d in ds:
            for col in range(2):
                h_copy(i, col, d).start()

    def p_first(n):
        ref = pair_v.at[zh, x * 2 + c]
        xx = (x, xr, xr, xl, xl, xo, xo)[n]
        cc = (1 - c, c, 1 - c, c, 1 - c, c, 1 - c)[n]
        return remote(ref, ref, p_ssem.at[0], p_rsem.at[0], dev(zl, y, xx, zh, cc))

    def p_second(d):
        ref = pack_v.at[zh]
        return remote(ref, ref, p_ssem.at[1], p_rsem.at[1], dev(zl, y, x, (zh + d) % 4, c))

    def p_step():
        landed(pair_v.at[0, pl.ds(0, 7)], p_rsem.at[0])
        lane = lax.broadcasted_iota(jnp.int32, (8, 128), 1)
        packed = pair_v[zh, 0]
        for k in range(1, 8):
            packed = jnp.where(lane >= 16 * k, pair_v[zh, k], packed)
        pack_v[zh] = packed
        for d in (2, 1, 3):
            p_second(d).start()

    pl.semaphore_wait(barrier, len(peers))
    for n in range(7):
        p_first(n).start()
    rot_copy.wait()
    const_copies = (
        pltpu.make_async_copy(spread_ref, spread_v, c_sem.at[0]),
        pltpu.make_async_copy(mask_ref, mask_v, c_sem.at[1]),
    )
    for copy in const_copies:
        copy.start()
    for i in range(1, ROUNDS):
        df_copy(i).start()
    half_step(0)
    half_send(0)
    p_step()
    half_step(1)
    half_send(1, FIRST if 1 in LATE else FIRST + SECOND)

    def p_last_step():
        landed(pack_v.at[pl.ds(0, 3)], p_rsem.at[1])

    p_last_step()

    def w_step():
        blocks = [
            [jnp.broadcast_to(pack_v[z][:, 16 * k : 16 * k + 1], (8, 128)) for k in range(8)] for z in range(4)
        ]
        for col in range(2):
            u, j, xh, pq = place(col)
            wanted = jnp.concatenate(
                [blocks[(z + 1 + col) % 4][(2 * h + jj + col) % 4 * 2 + cc] for h in range(2) for z in range(4) for jj in range(2) for cc in range(2)],
                axis=0,
            )
            at = lax.broadcasted_iota(jnp.int32, wanted.shape, 1)
            for n in range(natural // 128):
                hot_v[:, n * 128 : (n + 1) * 128] = jnp.where(wanted == at + n * 128, 1.0, 0.0).astype(BF)
            total = None
            for jj in range(2):
                xs = (xh * 2 + jj + col) % 4
                rows = rot_v[pl.ds(pl.multiple_of((xs * 4 + zh) * 80, 16), 80)]
                sel = dot_nt(hot_v[...], rows).astype(BF)
                part = dot(sel, spread_v[jj])
                total = part if total is None else total + part
            w_v[col] = (total * mask_v[...].astype(F32)).astype(BF)

    for copy in const_copies:
        copy.wait()
    w_step()

    def zplace(col):
        uz = (zh + 4 - col) % 4
        return uz, (uz + 3) % 4

    def x_partner(col):
        return dev(zl, y, jnp.where(place(col)[1] == 1, xr, xl), zh, c)

    def z_partner(col):
        uz, p = zplace(col)
        return dev(zl, y, x, (uz + 1 - 2 * (uz % 2) + col) % 4, c)

    def t_copy(i, col, n):
        to = z_partner(col) if i in Z_FIRST else x_partner(col)
        at = pl.ds(*pieces(i)[n])
        return remote(tsend_v.at[i, col, :, at], trecv_v.at[i, col, :, at], t_ssem, t_rsem.at[i, col, n], to)

    def w_rows(i, col, own):
        xh, s = place(col)[2], zplace(col)[1] // 2
        if i not in Z_FIRST:
            return w_v[col, pl.ds(pl.multiple_of((xh if own else 1 - xh) * 128, 128), 128)]
        s = s if own else 1 - s
        return jnp.concatenate([w_v[col, pl.ds(pl.multiple_of((2 * h + s) * 64, 64), 64)] for h in range(2)], axis=0)

    def t_step(i, col, n):
        if n == 0:
            landed(quad_v.at[i, col], h_rsem.at[i, col])
        at = pl.ds(*pieces(i)[n])
        tsend_v[i, col, :, at] = dot(w_rows(i, col, False), quad_v[i, col, :, at]).astype(BF)
        t_copy(i, col, n).start()
        town_v[i, col, :, at] = dot(w_rows(i, col, True), quad_v[i, col, :, at])

    def a_copy(i, col, n):
        to = x_partner(col) if i in Z_FIRST else z_partner(col)
        at = pl.ds(*pieces(i)[n])
        return remote(asend_v.at[i, col, :, at], arecv_v.at[i, col, :, at], a_ssem, a_rsem.at[i, col, n], to)

    def a_step(i, col, n):
        t_copy(i, col, n).wait_recv()
        half = place(col)[2] if i in Z_FIRST else zplace(col)[1] // 2
        at = pl.ds(*pieces(i)[n])
        other = pl.ds(pl.multiple_of((1 - half) * 64, 64), 64)
        own = pl.ds(pl.multiple_of(half * 64, 64), 64)
        asend_v[i, col, :, at] = (town_v[i, col, other, at] + trecv_v[i, col, other, at].astype(F32)).astype(BF)
        a_copy(i, col, n).start()
        aown_v[i, col, :, at] = town_v[i, col, own, at] + trecv_v[i, col, own, at].astype(F32)

    def b_copy(i, col, n):
        uz, p = zplace(col)
        zd = (p + 2 - 2 * (p % 2) + col) % 4
        at = pl.ds(*pieces(i)[n])
        return remote(
            bsend_v.at[i, col, :, at], brecv_v.at[i, col, :, at], b_ssem, b_rsem.at[i, col, n], dev(zl, y, x, zd, c)
        )

    def b_step(i, col, n):
        a_copy(i, col, n).wait_recv()
        uz, p = zplace(col)
        at = pl.ds(*pieces(i)[n])
        other = pl.ds(pl.multiple_of((1 - p % 2) * 32, 32), 32)
        own = pl.ds(pl.multiple_of(p % 2 * 32, 32), 32)
        bsend_v[i, col, :, at] = (aown_v[i, col, other, at] + arecv_v[i, col, other, at].astype(F32)).astype(BF)
        b_copy(i, col, n).start()
        bown_v[i, col, :, at] = aown_v[i, col, own, at] + arecv_v[i, col, own, at].astype(F32)

    def g_copy(i, col, d):
        u, j, xh, pq = place(col)
        slot = (zl * 2 + j) * 2 + c
        to = (slot + d) % 8
        zd, jd, cd = to // 4, (to // 2) % 2, to % 2
        src = gsend_v.at[i, col, zd, pl.ds(pl.multiple_of((jd * 2 + cd) * 16, 16), 16)]
        dst = gath_v.at[i * 2 + col, pl.ds(pl.multiple_of(slot * 16, 16), 16)]
        if d == 0:
            return pltpu.make_async_copy(src, dst, g_rsem.at[i, col])
        return remote(src, dst, g_ssem, g_rsem.at[i, col], dev(zd, y, (xh * 2 + jd + col) % 4, zh, cd))

    def f_step(i, col):
        for n in range(len(pieces(i))):
            b_copy(i, col, n).wait_recv()
        value = bown_v[i, col] + brecv_v[i, col].astype(F32)
        tiles = [value[:, 128 * n : 128 * (n + 1)] for n in range(5)]
        lower = lax.broadcasted_iota(jnp.int32, (32, 128), 0) % 8 >= 4
        for w in range(2):
            win, rest = tiles[2 * w : 2 * w + 3], (tiles[3:] if w == 0 else tiles[:2])
            shared = jnp.where(lower, rest[0], pltpu.roll(rest[1], 28, 0))
            upper = jnp.concatenate([win[0], win[1]], axis=1).reshape(4, 8, 256)
            under = jnp.concatenate([win[2], shared], axis=1).reshape(4, 8, 256)
            gsend_v[i, col, w] = jnp.concatenate([upper, under], axis=1).reshape(64, 256).astype(BF)
        for d in (4, 5, 6, 7, 2, 3, 1, 0):
            g_copy(i, col, d).start()

    def y_copy(i, col, d):
        return remote(
            ysend_v.at[i, col, d - 1], rows_v.at[y, i, col],
            y_ssem, y_rsem.at[i], dev(zl, (y + d) % 4, x, zh, c),
        )

    def y_step(i, col):
        landed(gath_v.at[i * 2 + col], g_rsem.at[i, col])
        packed = gath_v[i * 2 + col]
        upper = dot(order_v[0], packed).astype(BF)
        under = dot(order_v[1], packed).astype(BF)
        win = [upper[:32, :128], upper[:32, 128:], under[:32, :128]]
        rest = [under[:32, 128:], under[32:, 128:]]
        right = jnp.where(zl == 0, jnp.concatenate(win + rest, axis=1), jnp.concatenate(rest + win, axis=1))
        pick_copy = dot(jnp.concatenate([upper[32:], under[32:, :128]], axis=1), pick_v[...]).astype(BF)
        lefts = [pick_copy[:, 128 * n : 128 * (n + 1)] for n in range(4)]
        for d in (2, 1, 3, 0):
            to = (y + d) % 4
            left = jnp.where(to < 2, jnp.where(to == 0, lefts[0], lefts[1]), jnp.where(to == 2, lefts[2], lefts[3]))
            if d:
                ysend_v[i, col, d - 1, :, :natural] = right
                ysend_v[i, col, d - 1, :, natural:] = left
                y_copy(i, col, d).start()
            else:
                rows_v[y, i, col, :, :natural] = right
                rows_v[y, i, col, :, natural:] = left

    def out_step(i):
        landed(rows_v.at[pl.ds(0, 3), i], y_rsem.at[i])
        both = rows_v[:, i].reshape(256, natural + 128)
        left = both[:, natural:]
        parity = lax.broadcasted_iota(jnp.int32, left.shape, 0) % 2
        zero = jnp.zeros_like(left)
        left = jnp.concatenate([jnp.where(parity == t, left, zero) for t in range(2)], axis=1)
        acc_v[...] += lax.dot_general(
            left, both[:, :natural], (((0,), (0,)), ((), ())), preferred_element_type=F32
        )

    def one_hots():
        to = lax.broadcasted_iota(jnp.int32, (64, 128), 0)
        at = lax.broadcasted_iota(jnp.int32, (64, 128), 1)
        source = (to % 32) // 4 * 16 + to % 4 + jnp.where(to < 32, 4, 0)
        for n in range(2):
            order_v[n] = jnp.where(at == source + 8 * n, 1.0, 0.0).astype(BF)
        at = lax.broadcasted_iota(jnp.int32, (384, 512), 0)
        to = lax.broadcasted_iota(jnp.int32, (384, 512), 1)
        source = (zl * 4 + to // 128) * 80 + to % 128 - zl * 256
        pick_v[...] = jnp.where((at == source) & (to % 128 < 80), 1.0, 0.0).astype(BF)
        acc_v[...] = jnp.zeros_like(acc_v)

    def drain_step():
        landed(pair_v.at[0, pl.ds(0, 7)], p_ssem.at[0])
        landed(pack_v.at[pl.ds(0, 3)], p_ssem.at[1])
        landed(half_v.at[pl.ds(0, 3)], h_ssem)
        landed(tsend_v, t_ssem)
        landed(asend_v, a_ssem)
        landed(bsend_v, b_ssem)
        landed(gath_v.at[pl.ds(0, 2 * ROUNDS - 1)], g_ssem)

    steps = {"t": t_step, "a": a_step, "b": b_step, "f": f_step, "y": y_step}
    one_hots()
    for token in PLAN:
        name, i = token[0], int(token[1])
        if name == "h":
            half_step(i)
            half_send(i, FIRST if i in LATE else FIRST + SECOND)
        elif name == "s":
            half_send(i, SECOND)
        elif name == "o":
            out_step(i)
        elif name == "d":
            drain_step()
        elif name in "tab":
            for n in (int(token[2]),) if len(token) > 2 else range(len(pieces(i))):
                for col in range(2):
                    steps[name](i, col, n)
        else:
            for col in range(2):
                steps[name](i, col)

    def out_copy(t, n):
        rows = 80 // 1
        return pltpu.make_async_copy(
            acc_v.at[pl.ds(128 * t + n * rows, rows)],
            out_ref.at[pl.ds(n * rows, rows), pl.ds(natural * t, natural)],
            o_sem.at[t],
        )

    def w_out_step():
        for t in range(2):
            for n in range(1):
                out_copy(t, n).start()
        for t in range(2):
            for n in range(1):
                out_copy(t, n).wait()

    w_out_step()
    landed(ysend_v, y_ssem)


def constants():
    k = np.arange(4 * SUB * 40)
    dev, fun, orb = k // (SUB * 40), (k // 40) % SUB, k % 40
    a = np.arange(80)
    spread = np.stack(
        [(dev[None] == 2 * jj + a[:, None] // 40) & (orb[None] == a[:, None] % 40) for jj in range(2)]
    )
    r = np.arange(256)
    mask = ((r[:, None] // 2) % SUB) == fun[None]
    return spread.astype(np.float32), mask.astype(np.float32)


def solution(mesh):
    spread, mask = constants()

    def local(df_blocks, fno_rotation, tile_pairs):
        aux_n, orbs, nv = df_blocks.shape
        nf = fno_rotation.shape[1]
        rows = aux_n * orbs // ROUNDS
        vm = pltpu.VMEM
        dma = pltpu.SemaphoreType.DMA
        out = pl.pallas_call(
            kernel,
            name="tiles",
            out_shape=jax.ShapeDtypeStruct((80, 2 * nf), F32),
            in_specs=[
                pl.BlockSpec(memory_space=pl.ANY),
                pl.BlockSpec(memory_space=pl.ANY),
                pl.BlockSpec(memory_space=pltpu.SMEM),
                pl.BlockSpec(memory_space=pl.ANY),
                pl.BlockSpec(memory_space=pl.ANY),
            ],
            out_specs=pl.BlockSpec(memory_space=pl.ANY),
            scratch_shapes=[
                vm((2, 80, 4 * SUB * 40), BF),
                vm((256, 4 * SUB * 40), BF),
                vm((ROUNDS, rows, nv), BF),
                vm((nv, nf), BF),
                vm((ROUNDS, rows, nf), BF),
                vm((ROUNDS, 2, rows // 2, nf), BF),
                vm((4, 8, 8, 128), jnp.int32),
                vm((4, 8, 128), jnp.int32),
                vm((256, nf), BF),
                vm((2, 256, 4 * SUB * 40), BF),
                vm((ROUNDS, 2, 128, nf), BF),
                vm((ROUNDS, 2, 128, nf), F32),
                vm((ROUNDS, 2, 128, nf), BF),
                vm((ROUNDS, 2, 64, nf), BF),
                vm((ROUNDS, 2, 64, nf), F32),
                vm((ROUNDS, 2, 64, nf), BF),
                vm((ROUNDS, 2, 32, nf), BF),
                vm((ROUNDS, 2, 32, nf), F32),
                vm((ROUNDS, 2, 32, nf), BF),
                vm((ROUNDS, 2, 2, 64, 256), BF),
                vm((ROUNDS * 2, 128, 256), BF),
                vm((2, 64, 128), BF),
                vm((384, 512), BF),
                vm((4, ROUNDS, 2, 32, nf + 128), BF),
                vm((ROUNDS, 2, 3, 32, nf + 128), BF),
                vm((256, nf), F32),
                dma((2,)),
                dma((ROUNDS,)),
                dma(()),
                dma((2,)), dma((2,)),
                dma(()), dma((ROUNDS, 2)),
                dma(()), dma((ROUNDS, 2, 2)),
                dma(()), dma((ROUNDS, 2, 2)),
                dma(()), dma((ROUNDS, 2, 2)),
                dma(()), dma((ROUNDS, 2)),
                dma(()), dma((ROUNDS,)),
                dma((2,)),
            ],
            compiler_params=pltpu.CompilerParams(
                collective_id=0, has_side_effects=True, vmem_limit_bytes=59392 * 2**10
            ),
        )(
            df_blocks.reshape(aux_n * orbs, nv),
            fno_rotation,
            tile_pairs,
            jnp.asarray(spread, BF),
            jnp.asarray(mask, BF),
        )
        return out.reshape(80, 2, nf)

    placed = (P("aux", "virt", None), P(), P("virt", None))
    return jax.shard_map(local, mesh=mesh, in_specs=placed, out_specs=P("aux", "virt", None), check_vma=False)
```

```python
import jax
import jax.numpy as jnp
import numpy as np
from jax import lax
from jax.experimental import pallas as pl
from jax.experimental.pallas import tpu as pltpu
from jax.sharding import PartitionSpec as P

MESH = pl.DeviceIdType.MESH
BF = jnp.bfloat16
F32 = jnp.float32

ROUNDS = 4
Z_ROUNDS = (1,)
FIRST, SECOND = (2, 1, 0), (3,)
LATE = (2,)
SPLIT = (0, 1, 2, 3)
PLAN = (
    "h0", "h3", "p0", "h1", "w0", "t0", "h2", "t3", "a0", "s2", "b0", "a3", "w1", "t2", "c0", "f0", "t1",
    "b3", "a2", "f3", "y0", "a1", "b2", "b1", "y3", "f2", "f1", "o0", "y2", "o3", "y1", "o2", "d0", "o1",
)
SUB = 2


def pieces(i):
    return ((0, 384), (384, 256)) if i in SPLIT else ((0, 640),)


def dot(a, b):
    return jnp.dot(a, b, preferred_element_type=F32)


def dot_nt(a, b):
    return lax.dot_general(a, b, (((1,), (1,)), ((), ())), preferred_element_type=F32)


def kernel(
    df_ref, rot_ref, pairs_ref, spread_ref, mask_ref, out_ref,
    spread_v, mask_v, df_v, rot_v, half_v, quad_v, pair_v, pack_v, hot_v, w_v, tsend_v, town_v, trecv_v,
    asend_v, aown_v, arecv_v, bsend_v, bown_v, brecv_v, gsend_v, gath_v, order_v, pick_v, rows_v, ysend_v, acc_v,
    c_sem, df_sem, rot_sem, p_ssem, p_rsem, h_ssem, h_rsem, t_ssem, t_rsem,
    a_ssem, a_rsem, b_ssem, b_rsem, g_ssem, g_rsem, y_ssem, y_rsem, o_sem,
):
    natural = rot_v.shape[1]
    aux = lax.axis_index("aux")
    virt = lax.axis_index("virt")
    zl, y = aux // 4, aux % 4
    x, zh, c = virt // 8, (virt // 2) % 4, virt % 2
    hrows = half_v.shape[1] // 8
    rrows = half_v.shape[1]

    def dev(zl_, y_, x_, zh_, c_):
        return (zl_ * 4 + y_, (x_ * 4 + zh_) * 2 + c_)

    def remote(src, dst, ssem, rsem, device):
        return pltpu.make_async_remote_copy(
            src_ref=src, dst_ref=dst, send_sem=ssem, recv_sem=rsem, device_id=device, device_id_type=MESH
        )

    def landed(ref, sem):
        pltpu.make_async_copy(ref, ref, sem).wait()

    def df_copy(i):
        return pltpu.make_async_copy(df_ref.at[pl.ds(i * rrows, rrows)], df_v.at[i], df_sem.at[i])

    rot_copy = pltpu.make_async_copy(rot_ref, rot_v, rot_sem)
    rot_copy.start()
    df_copy(0).start()

    xr, xl = (x + 1) % 4, (x + 3) % 4
    xo = (x + 2) % 4
    peers = [dev(zl, y, x, zh, 1 - c)]
    peers += [dev(zl, y, xx, zh, cc) for xx in (xr, xl, xo) for cc in range(2)]
    peers += [dev(zl, y, x, (zh + d) % 4, c) for d in range(1, 4)]
    peers += [dev(zl, y, x, (zh + d) % 4, 1 - c) for d in (1, 3)]
    peers += [dev(1 - zl, y, x, (zh + d) % 4, cc) for d in (1, 3) for cc in range(2)]
    peers += [dev(1 - zl, y, xx, zh, cc) for xx in (x, xr, xl) for cc in range(2)]
    peers += [dev(zl, (y + d) % 4, x, zh, c) for d in range(1, 4)]
    barrier = pltpu.get_barrier_semaphore()
    for peer in peers:
        pl.semaphore_signal(barrier, inc=1, device_id=peer, device_id_type=MESH)

    row = lax.broadcasted_iota(jnp.int32, (8, 128), 0)
    tile = row % 2
    side = row // 4
    mine = jnp.where(
        side == 0,
        jnp.where(tile == 0, pairs_ref[0, 0], pairs_ref[1, 0]),
        jnp.where(tile == 0, pairs_ref[0, 1], pairs_ref[1, 1]),
    )
    pair_v[zh, x * 2 + c] = mine

    def to_ring(i, first, second, core, zl_=zl):
        return dev(zl_, y, second, first, core) if i in Z_ROUNDS else dev(zl_, y, first, second, core)

    def place(i, col):
        first, second = (zh, x) if i in Z_ROUNDS else (x, zh)
        u, v = (first + 4 - col) % 4, (second + 4 - col) % 4
        p = (v + 3) % 4
        return first, second, u % 2, u // 2, (u % 2 + u // 2) % 2, v, p

    def stage(i, col, n):
        first, second, j, s1, pq, v, p = place(i, col)
        n = (n + 1) % 3 if i in Z_ROUNDS else n
        if n == 0:
            return s1, to_ring(i, (first + jnp.where(j == 1, 1, 3)) % 4, second, c)
        if n == 1:
            return p // 2, to_ring(i, first, (v + 1 - 2 * (v % 2) + col) % 4, c)
        return p % 2, to_ring(i, first, (p + 2 - 2 * (p % 2) + col) % 4, c)

    def h_copy(i, col, d):
        first, second, j, s1, pq, v, p = place(i, col)
        q, cd = (pq + d // 2) % 2, (c + d % 2) % 2
        fd = (s1 * 2 + (q + s1) % 2 + col) % 4
        src = half_v.at[i, pl.ds(pl.multiple_of(col * 4 * hrows + (q * 2 + cd) * hrows, 16), hrows)]
        dst = quad_v.at[i, col, pl.ds(pl.multiple_of((j * 2 + c) * hrows, 16), hrows)]
        if d == 0:
            return pltpu.make_async_copy(src, dst, h_rsem.at[i, col])
        return remote(src, dst, h_ssem, h_rsem.at[i, col], to_ring(i, fd, second, cd))

    def half_step(i):
        df_copy(i).wait()
        half_v[i] = dot(df_v[i], rot_v[...]).astype(BF)

    def half_send(i, ds=(2, 3, 1, 0)):
        for d in ds:
            for col in range(2):
                h_copy(i, col, d).start()

    def p_first(n):
        ref = pair_v.at[zh, x * 2 + c]
        xx = (x, xr, xr, xl, xl, xo, xo)[n]
        cc = (1 - c, c, 1 - c, c, 1 - c, c, 1 - c)[n]
        return remote(ref, ref, p_ssem.at[0], p_rsem.at[0], dev(zl, y, xx, zh, cc))

    def p_second(d):
        ref = pack_v.at[zh]
        return remote(ref, ref, p_ssem.at[1], p_rsem.at[1], dev(zl, y, x, (zh + d) % 4, c))

    def p_step():
        landed(pair_v.at[0, pl.ds(0, 7)], p_rsem.at[0])
        lane = lax.broadcasted_iota(jnp.int32, (8, 128), 1)
        packed = pair_v[zh, 0]
        for k in range(1, 8):
            packed = jnp.where(lane >= 16 * k, pair_v[zh, k], packed)
        pack_v[zh] = packed
        for d in (2, 1, 3):
            p_second(d).start()

    pl.semaphore_wait(barrier, len(peers))
    for n in range(7):
        p_first(n).start()
    rot_copy.wait()
    const_copies = (
        pltpu.make_async_copy(spread_ref, spread_v, c_sem.at[0]),
        pltpu.make_async_copy(mask_ref, mask_v, c_sem.at[1]),
    )
    for copy in const_copies:
        copy.start()
    for i in range(1, ROUNDS):
        df_copy(i).start()

    def w_step(i):
        if i == 0:
            landed(pack_v.at[pl.ds(0, 3)], p_rsem.at[1])
            for copy in const_copies:
                copy.wait()
        blocks = [
            [jnp.broadcast_to(pack_v[z][:, 16 * k : 16 * k + 1], (8, 128)) for k in range(8)] for z in range(4)
        ]
        two = range(2)
        for col in range(2):
            first, second, j, s1, pq, v, p = place(i, col)
            if i in Z_ROUNDS:
                order = [
                    ((2 * h + jj + col) % 4, (2 * s2 + s3 + 1 + col) % 4, cc)
                    for s2 in two for s3 in two for h in two for jj in two for cc in two
                ]
            else:
                order = [
                    ((2 * s2 + s3 + 1 + col) % 4, (2 * h + jj + col) % 4, cc)
                    for h in two for s2 in two for s3 in two for jj in two for cc in two
                ]
            wanted = jnp.concatenate([blocks[z][xx * 2 + cc] for z, xx, cc in order], axis=0)
            at = lax.broadcasted_iota(jnp.int32, wanted.shape, 1)
            for n in range(natural // 128):
                hot_v[:, n * 128 : (n + 1) * 128] = jnp.where(wanted == at + n * 128, 1.0, 0.0).astype(BF)
            total = None
            for jj in two:
                fs = (s1 * 2 + jj + col) % 4
                chip = x * 4 + fs if i in Z_ROUNDS else fs * 4 + zh
                sel = dot_nt(hot_v[...], rot_v[pl.ds(pl.multiple_of(chip * 80, 16), 80)]).astype(BF)
                part = dot(sel, spread_v[jj])
                total = part if total is None else total + part
            w_v[kind(i) * 2 + col] = (total * mask_v[...].astype(F32)).astype(BF)

    def kind(i):
        return 1 if i in Z_ROUNDS else 0

    def half_rows(half, size):
        return pl.ds(pl.multiple_of(half * size, size), size)

    def t_copy(i, col, n):
        at = pl.ds(*pieces(i)[n])
        return remote(
            tsend_v.at[i, col, :, at], trecv_v.at[i, col, :, at], t_ssem, t_rsem.at[i, col, n], stage(i, col, 0)[1]
        )

    def t_step(i, col, n):
        if n == 0:
            landed(quad_v.at[i, col], h_rsem.at[i, col])
        at = pl.ds(*pieces(i)[n])
        half = stage(i, col, 0)[0]
        w = w_v.at[kind(i) * 2 + col]
        tsend_v[i, col, :, at] = dot(w[half_rows(1 - half, 128)], quad_v[i, col, :, at]).astype(BF)
        t_copy(i, col, n).start()
        town_v[i, col, :, at] = dot(w[half_rows(half, 128)], quad_v[i, col, :, at])

    def a_copy(i, col, n):
        at = pl.ds(*pieces(i)[n])
        return remote(
            asend_v.at[i, col, :, at], arecv_v.at[i, col, :, at], a_ssem, a_rsem.at[i, col, n], stage(i, col, 1)[1]
        )

    def a_step(i, col, n):
        t_copy(i, col, n).wait_recv()
        at = pl.ds(*pieces(i)[n])
        half = stage(i, col, 1)[0]
        other, own = half_rows(1 - half, 64), half_rows(half, 64)
        asend_v[i, col, :, at] = (town_v[i, col, other, at] + trecv_v[i, col, other, at].astype(F32)).astype(BF)
        a_copy(i, col, n).start()
        aown_v[i, col, :, at] = town_v[i, col, own, at] + trecv_v[i, col, own, at].astype(F32)

    def b_copy(i, col, n):
        at = pl.ds(*pieces(i)[n])
        return remote(
            bsend_v.at[i, col, :, at], brecv_v.at[i, col, :, at], b_ssem, b_rsem.at[i, col, n], stage(i, col, 2)[1]
        )

    def b_step(i, col, n):
        a_copy(i, col, n).wait_recv()
        at = pl.ds(*pieces(i)[n])
        half = stage(i, col, 2)[0]
        other, own = half_rows(1 - half, 32), half_rows(half, 32)
        bsend_v[i, col, :, at] = (aown_v[i, col, other, at] + arecv_v[i, col, other, at].astype(F32)).astype(BF)
        b_copy(i, col, n).start()
        bown_v[i, col, :, at] = aown_v[i, col, own, at] + arecv_v[i, col, own, at].astype(F32)

    def g_copy(i, col, d):
        first, second, j, s1, pq, v, p = place(i, col)
        slot = (zl * 2 + j) * 2 + c
        to = (slot + d) % 8
        zd, jd, cd = to // 4, (to // 2) % 2, to % 2
        src = gsend_v.at[i, col, zd, pl.ds(pl.multiple_of((jd * 2 + cd) * 16, 16), 16)]
        dst = gath_v.at[i * 2 + col, pl.ds(pl.multiple_of(slot * 16, 16), 16)]
        if d == 0:
            return pltpu.make_async_copy(src, dst, g_rsem.at[i, col])
        return remote(src, dst, g_ssem, g_rsem.at[i, col], to_ring(i, (s1 * 2 + jd + col) % 4, second, cd, zd))

    def f_step(i, col):
        for n in range(len(pieces(i))):
            b_copy(i, col, n).wait_recv()
        value = bown_v[i, col] + brecv_v[i, col].astype(F32)
        tiles = [value[:, 128 * n : 128 * (n + 1)] for n in range(5)]
        lower = lax.broadcasted_iota(jnp.int32, (32, 128), 0) % 8 >= 4
        for w in range(2):
            win, rest = tiles[2 * w : 2 * w + 3], (tiles[3:] if w == 0 else tiles[:2])
            shared = jnp.where(lower, rest[0], pltpu.roll(rest[1], 28, 0))
            upper = jnp.concatenate([win[0], win[1]], axis=1).reshape(4, 8, 256)
            under = jnp.concatenate([win[2], shared], axis=1).reshape(4, 8, 256)
            gsend_v[i, col, w] = jnp.concatenate([upper, under], axis=1).reshape(64, 256).astype(BF)
        for d in (4, 5, 6, 7, 2, 3, 1, 0):
            g_copy(i, col, d).start()

    def y_copy(i, col, d):
        return remote(
            ysend_v.at[i, col, d - 1], rows_v.at[y, i, col],
            y_ssem, y_rsem.at[i], dev(zl, (y + d) % 4, x, zh, c),
        )

    def y_step(i, col):
        landed(gath_v.at[i * 2 + col], g_rsem.at[i, col])
        packed = gath_v[i * 2 + col]
        upper = dot(order_v[0], packed).astype(BF)
        under = dot(order_v[1], packed).astype(BF)
        win = [upper[:32, :128], upper[:32, 128:], under[:32, :128]]
        rest = [under[:32, 128:], under[32:, 128:]]
        right = jnp.where(zl == 0, jnp.concatenate(win + rest, axis=1), jnp.concatenate(rest + win, axis=1))
        pick_copy = dot(jnp.concatenate([upper[32:], under[32:, :128]], axis=1), pick_v[...]).astype(BF)
        lefts = [pick_copy[:, 128 * n : 128 * (n + 1)] for n in range(4)]
        for d in (2, 1, 3, 0):
            to = (y + d) % 4
            left = jnp.where(to < 2, jnp.where(to == 0, lefts[0], lefts[1]), jnp.where(to == 2, lefts[2], lefts[3]))
            if d:
                ysend_v[i, col, d - 1, :, :natural] = right
                ysend_v[i, col, d - 1, :, natural:] = left
                y_copy(i, col, d).start()
            else:
                rows_v[y, i, col, :, :natural] = right
                rows_v[y, i, col, :, natural:] = left

    def out_step(i):
        landed(rows_v.at[pl.ds(0, 3), i], y_rsem.at[i])
        both = rows_v[:, i].reshape(256, natural + 128)
        left = both[:, natural:]
        parity = lax.broadcasted_iota(jnp.int32, left.shape, 0) % 2
        zero = jnp.zeros_like(left)
        left = jnp.concatenate([jnp.where(parity == t, left, zero) for t in range(2)], axis=1)
        acc_v[...] += lax.dot_general(
            left, both[:, :natural], (((0,), (0,)), ((), ())), preferred_element_type=F32
        )

    def one_hots():
        to = lax.broadcasted_iota(jnp.int32, (64, 128), 0)
        at = lax.broadcasted_iota(jnp.int32, (64, 128), 1)
        source = (to % 32) // 4 * 16 + to % 4 + jnp.where(to < 32, 4, 0)
        for n in range(2):
            order_v[n] = jnp.where(at == source + 8 * n, 1.0, 0.0).astype(BF)
        at = lax.broadcasted_iota(jnp.int32, (384, 512), 0)
        to = lax.broadcasted_iota(jnp.int32, (384, 512), 1)
        source = (zl * 4 + to // 128) * 80 + to % 128 - zl * 256
        pick_v[...] = jnp.where((at == source) & (to % 128 < 80), 1.0, 0.0).astype(BF)
        acc_v[...] = jnp.zeros_like(acc_v)

    def drain_step():
        landed(pair_v.at[0, pl.ds(0, 7)], p_ssem.at[0])
        landed(pack_v.at[pl.ds(0, 3)], p_ssem.at[1])
        landed(half_v.at[pl.ds(0, 3)], h_ssem)
        landed(tsend_v, t_ssem)
        landed(asend_v, a_ssem)
        landed(bsend_v, b_ssem)
        landed(gath_v.at[pl.ds(0, 2 * ROUNDS - 1)], g_ssem)

    steps = {"t": t_step, "a": a_step, "b": b_step, "f": f_step, "y": y_step}
    for token in PLAN:
        name, i = token[0], int(token[1])
        if name == "h":
            half_step(i)
            half_send(i, FIRST if i in LATE else FIRST + SECOND)
        elif name == "s":
            half_send(i, SECOND)
        elif name == "o":
            out_step(i)
        elif name == "d":
            drain_step()
        elif name == "p":
            p_step()
        elif name == "w":
            w_step(i)
        elif name == "c":
            one_hots()
        elif name in "tab":
            for n in (int(token[2]),) if len(token) > 2 else range(len(pieces(i))):
                for col in range(2):
                    steps[name](i, col, n)
        else:
            for col in range(2):
                steps[name](i, col)

    def out_copy(t, n):
        rows = 80 // 1
        return pltpu.make_async_copy(
            acc_v.at[pl.ds(128 * t + n * rows, rows)],
            out_ref.at[pl.ds(n * rows, rows), pl.ds(natural * t, natural)],
            o_sem.at[t],
        )

    def w_out_step():
        for t in range(2):
            for n in range(1):
                out_copy(t, n).start()
        for t in range(2):
            for n in range(1):
                out_copy(t, n).wait()

    w_out_step()
    landed(ysend_v, y_ssem)


def constants():
    k = np.arange(4 * SUB * 40)
    dev, fun, orb = k // (SUB * 40), (k // 40) % SUB, k % 40
    a = np.arange(80)
    spread = np.stack(
        [(dev[None] == 2 * jj + a[:, None] // 40) & (orb[None] == a[:, None] % 40) for jj in range(2)]
    )
    r = np.arange(256)
    mask = ((r[:, None] // 2) % SUB) == fun[None]
    return spread.astype(np.float32), mask.astype(np.float32)


def solution(mesh):
    spread, mask = constants()

    def local(df_blocks, fno_rotation, tile_pairs):
        aux_n, orbs, nv = df_blocks.shape
        nf = fno_rotation.shape[1]
        rows = aux_n * orbs // ROUNDS
        vm = pltpu.VMEM
        dma = pltpu.SemaphoreType.DMA
        out = pl.pallas_call(
            kernel,
            name="tiles",
            out_shape=jax.ShapeDtypeStruct((80, 2 * nf), F32),
            in_specs=[
                pl.BlockSpec(memory_space=pl.ANY),
                pl.BlockSpec(memory_space=pl.ANY),
                pl.BlockSpec(memory_space=pltpu.SMEM),
                pl.BlockSpec(memory_space=pl.ANY),
                pl.BlockSpec(memory_space=pl.ANY),
            ],
            out_specs=pl.BlockSpec(memory_space=pl.ANY),
            scratch_shapes=[
                vm((2, 80, 4 * SUB * 40), BF),
                vm((256, 4 * SUB * 40), BF),
                vm((ROUNDS, rows, nv), BF),
                vm((nv, nf), BF),
                vm((ROUNDS, rows, nf), BF),
                vm((ROUNDS, 2, rows // 2, nf), BF),
                vm((4, 8, 8, 128), jnp.int32),
                vm((4, 8, 128), jnp.int32),
                vm((256, nf), BF),
                vm((4, 256, 4 * SUB * 40), BF),
                vm((ROUNDS, 2, 128, nf), BF),
                vm((ROUNDS, 2, 128, nf), F32),
                vm((ROUNDS, 2, 128, nf), BF),
                vm((ROUNDS, 2, 64, nf), BF),
                vm((ROUNDS, 2, 64, nf), F32),
                vm((ROUNDS, 2, 64, nf), BF),
                vm((ROUNDS, 2, 32, nf), BF),
                vm((ROUNDS, 2, 32, nf), F32),
                vm((ROUNDS, 2, 32, nf), BF),
                vm((ROUNDS, 2, 2, 64, 256), BF),
                vm((ROUNDS * 2, 128, 256), BF),
                vm((2, 64, 128), BF),
                vm((384, 512), BF),
                vm((4, ROUNDS, 2, 32, nf + 128), BF),
                vm((ROUNDS, 2, 3, 32, nf + 128), BF),
                vm((256, nf), F32),
                dma((2,)),
                dma((ROUNDS,)),
                dma(()),
                dma((2,)), dma((2,)),
                dma(()), dma((ROUNDS, 2)),
                dma(()), dma((ROUNDS, 2, 3)),
                dma(()), dma((ROUNDS, 2, 3)),
                dma(()), dma((ROUNDS, 2, 3)),
                dma(()), dma((ROUNDS, 2)),
                dma(()), dma((ROUNDS,)),
                dma((2,)),
            ],
            compiler_params=pltpu.CompilerParams(
                collective_id=0, has_side_effects=True, vmem_limit_bytes=59392 * 2**10
            ),
        )(
            df_blocks.reshape(aux_n * orbs, nv),
            fno_rotation,
            tile_pairs,
            jnp.asarray(spread, BF),
            jnp.asarray(mask, BF),
        )
        return out.reshape(80, 2, nf)

    placed = (P("aux", "virt", None), P(), P("virt", None))
    return jax.shard_map(local, mesh=mesh, in_specs=placed, out_specs=P("aux", "virt", None), check_vma=False)
```

```python
import jax
import jax.numpy as jnp
import numpy as np
from jax import lax
from jax.experimental import pallas as pl
from jax.experimental.pallas import tpu as pltpu
from jax.sharding import PartitionSpec as P

MESH = pl.DeviceIdType.MESH
BF = jnp.bfloat16
F32 = jnp.float32

ROUNDS = 4
Z_ROUNDS = (1,)
FIRST, SECOND = (2, 1, 0), (3,)
LATE = (2,)
SPLIT = (0, 1, 2, 3)
PLAN = (
    "h3", "p0", "h1", "w0", "t0", "h2", "t3", "a0", "s2", "b0", "a3", "w1", "t2", "c0", "f0", "t1", "b3",
    "a2", "f3", "y0", "a1", "b2", "b1", "y3", "f2", "f1", "o0", "y2", "o3", "y1", "o2", "d0", "o1",
)
SUB = 2


def pieces(i):
    return ((0, 256), (256, 256), (512, 128)) if i in SPLIT else ((0, 640),)


def dot(a, b):
    return jnp.dot(a, b, preferred_element_type=F32)


def dot_nt(a, b):
    return lax.dot_general(a, b, (((1,), (1,)), ((), ())), preferred_element_type=F32)


def kernel(
    df_ref, rot_ref, pairs_ref, spread_ref, mask_ref, out_ref,
    spread_v, mask_v, df_v, rot_v, half_v, quad_v, pair_v, pack_v, hot_v, w_v, tsend_v, town_v, trecv_v,
    asend_v, aown_v, arecv_v, bsend_v, bown_v, brecv_v, gsend_v, gath_v, order_v, pick_v, rows_v, ysend_v, acc_v,
    c_sem, df_sem, rot_sem, p_ssem, p_rsem, h_ssem, h_rsem, t_ssem, t_rsem,
    a_ssem, a_rsem, b_ssem, b_rsem, g_ssem, g_rsem, y_ssem, y_rsem,
):
    natural = rot_v.shape[1]
    aux = lax.axis_index("aux")
    virt = lax.axis_index("virt")
    zl, y = aux // 4, aux % 4
    x, zh, c = virt // 8, (virt // 2) % 4, virt % 2
    hrows = half_v.shape[1] // 8
    rrows = half_v.shape[1]

    def dev(zl_, y_, x_, zh_, c_):
        return (zl_ * 4 + y_, (x_ * 4 + zh_) * 2 + c_)

    def remote(src, dst, ssem, rsem, device):
        return pltpu.make_async_remote_copy(
            src_ref=src, dst_ref=dst, send_sem=ssem, recv_sem=rsem, device_id=device, device_id_type=MESH
        )

    def landed(ref, sem):
        pltpu.make_async_copy(ref, ref, sem).wait()

    def df_copy(i):
        return pltpu.make_async_copy(df_ref.at[pl.ds(i * rrows, rrows)], df_v.at[i], df_sem.at[i])

    rot_copy = pltpu.make_async_copy(rot_ref, rot_v, rot_sem)
    rot_copy.start()
    df_copy(0).start()

    xr, xl = (x + 1) % 4, (x + 3) % 4
    xo = (x + 2) % 4
    peers = [dev(zl, y, x, zh, 1 - c)]
    peers += [dev(zl, y, xx, zh, cc) for xx in (xr, xl, xo) for cc in range(2)]
    peers += [dev(zl, y, x, (zh + d) % 4, c) for d in range(1, 4)]
    peers += [dev(zl, y, x, (zh + d) % 4, 1 - c) for d in (1, 3)]
    peers += [dev(1 - zl, y, x, (zh + d) % 4, cc) for d in (1, 3) for cc in range(2)]
    peers += [dev(1 - zl, y, xx, zh, cc) for xx in (x, xr, xl) for cc in range(2)]
    peers += [dev(zl, (y + d) % 4, x, zh, c) for d in range(1, 4)]
    barrier = pltpu.get_barrier_semaphore()
    for peer in peers:
        pl.semaphore_signal(barrier, inc=1, device_id=peer, device_id_type=MESH)

    row = lax.broadcasted_iota(jnp.int32, (8, 128), 0)
    tile = row % 2
    side = row // 4
    mine = jnp.where(
        side == 0,
        jnp.where(tile == 0, pairs_ref[0, 0], pairs_ref[1, 0]),
        jnp.where(tile == 0, pairs_ref[0, 1], pairs_ref[1, 1]),
    )
    pair_v[zh, x * 2 + c] = mine

    def to_ring(i, first, second, core, zl_=zl):
        return dev(zl_, y, second, first, core) if i in Z_ROUNDS else dev(zl_, y, first, second, core)

    def place(i, col):
        first, second = (zh, x) if i in Z_ROUNDS else (x, zh)
        u, v = (first + 4 - col) % 4, (second + 4 - col) % 4
        p = (v + 3) % 4
        return first, second, u % 2, u // 2, (u % 2 + u // 2) % 2, v, p

    def stage(i, col, n):
        first, second, j, s1, pq, v, p = place(i, col)
        n = (n + 1) % 3 if i in Z_ROUNDS else n
        if n == 0:
            return s1, to_ring(i, (first + jnp.where(j == 1, 1, 3)) % 4, second, c)
        if n == 1:
            return p // 2, to_ring(i, first, (v + 1 - 2 * (v % 2) + col) % 4, c)
        return p % 2, to_ring(i, first, (p + 2 - 2 * (p % 2) + col) % 4, c)

    def h_copy(i, col, d):
        first, second, j, s1, pq, v, p = place(i, col)
        q, cd = (pq + d // 2) % 2, (c + d % 2) % 2
        fd = (s1 * 2 + (q + s1) % 2 + col) % 4
        src = half_v.at[i, pl.ds(pl.multiple_of(col * 4 * hrows + (q * 2 + cd) * hrows, 16), hrows)]
        dst = quad_v.at[i, col, pl.ds(pl.multiple_of((j * 2 + c) * hrows, 16), hrows)]
        if d == 0:
            return pltpu.make_async_copy(src, dst, h_rsem.at[i, col])
        return remote(src, dst, h_ssem, h_rsem.at[i, col], to_ring(i, fd, second, cd))

    def half_step(i):
        df_copy(i).wait()
        for at in (pl.ds(0, rrows // 2), pl.ds(rrows // 2, rrows // 2)):
            for lo in range(0, natural, 256):
                to = pl.ds(lo, min(256, natural - lo))
                half_v[i, at, to] = dot(df_v[i, at], rot_v[:, to]).astype(BF)

    def half_send(i, ds=(2, 3, 1, 0)):
        for d in ds:
            for col in range(2):
                h_copy(i, col, d).start()

    def p_first(n):
        ref = pair_v.at[zh, x * 2 + c]
        xx = (x, xr, xr, xl, xl, xo, xo)[n]
        cc = (1 - c, c, 1 - c, c, 1 - c, c, 1 - c)[n]
        return remote(ref, ref, p_ssem.at[0], p_rsem.at[0], dev(zl, y, xx, zh, cc))

    def p_second(d):
        ref = pack_v.at[zh]
        return remote(ref, ref, p_ssem.at[1], p_rsem.at[1], dev(zl, y, x, (zh + d) % 4, c))

    def p_step():
        landed(pair_v.at[0, pl.ds(0, 7)], p_rsem.at[0])
        lane = lax.broadcasted_iota(jnp.int32, (8, 128), 1)
        packed = pair_v[zh, 0]
        for k in range(1, 8):
            packed = jnp.where(lane >= 16 * k, pair_v[zh, k], packed)
        pack_v[zh] = packed
        for d in (2, 1, 3):
            p_second(d).start()

    rot_copy.wait()
    const_copies = (
        pltpu.make_async_copy(spread_ref, spread_v, c_sem.at[0]),
        pltpu.make_async_copy(mask_ref, mask_v, c_sem.at[1]),
    )
    for copy in const_copies:
        copy.start()
    for i in range(1, ROUNDS):
        df_copy(i).start()

    half_step(0)
    pl.semaphore_wait(barrier, len(peers))
    for n in range(7):
        p_first(n).start()
    half_send(0)

    def w_step(i):
        if i == 0:
            landed(pack_v.at[pl.ds(0, 3)], p_rsem.at[1])
            for copy in const_copies:
                copy.wait()
        blocks = [
            [jnp.broadcast_to(pack_v[z][:, 16 * k : 16 * k + 1], (8, 128)) for k in range(8)] for z in range(4)
        ]
        two = range(2)
        for col in range(2):
            first, second, j, s1, pq, v, p = place(i, col)
            if i in Z_ROUNDS:
                order = [
                    ((2 * h + jj + col) % 4, (2 * s2 + s3 + 1 + col) % 4, cc)
                    for s2 in two for s3 in two for h in two for jj in two for cc in two
                ]
            else:
                order = [
                    ((2 * s2 + s3 + 1 + col) % 4, (2 * h + jj + col) % 4, cc)
                    for h in two for s2 in two for s3 in two for jj in two for cc in two
                ]
            wanted = jnp.concatenate([blocks[z][xx * 2 + cc] for z, xx, cc in order], axis=0)
            at = lax.broadcasted_iota(jnp.int32, wanted.shape, 1)
            for n in range(natural // 128):
                hot_v[:, n * 128 : (n + 1) * 128] = jnp.where(wanted == at + n * 128, 1.0, 0.0).astype(BF)
            total = None
            for jj in two:
                fs = (s1 * 2 + jj + col) % 4
                chip = x * 4 + fs if i in Z_ROUNDS else fs * 4 + zh
                sel = dot_nt(hot_v[...], rot_v[pl.ds(pl.multiple_of(chip * 80, 16), 80)]).astype(BF)
                part = dot(sel, spread_v[jj])
                total = part if total is None else total + part
            w_v[kind(i) * 2 + col] = (total * mask_v[...].astype(F32)).astype(BF)

    def kind(i):
        return 1 if i in Z_ROUNDS else 0

    def half_rows(half, size):
        return pl.ds(pl.multiple_of(half * size, size), size)

    def t_copy(i, col, n):
        at = pl.ds(*pieces(i)[n])
        return remote(
            tsend_v.at[i, col, :, at], trecv_v.at[i, col, :, at], t_ssem, t_rsem.at[i, col, n], stage(i, col, 0)[1]
        )

    def t_step(i, col, n):
        if n == 0:
            landed(quad_v.at[i, col], h_rsem.at[i, col])
        at = pl.ds(*pieces(i)[n])
        half = stage(i, col, 0)[0]
        w = w_v.at[kind(i) * 2 + col]
        tsend_v[i, col, :, at] = dot(w[half_rows(1 - half, 128)], quad_v[i, col, :, at]).astype(BF)
        t_copy(i, col, n).start()
        town_v[i, col, :, at] = dot(w[half_rows(half, 128)], quad_v[i, col, :, at])

    def a_copy(i, col, n):
        at = pl.ds(*pieces(i)[n])
        return remote(
            asend_v.at[i, col, :, at], arecv_v.at[i, col, :, at], a_ssem, a_rsem.at[i, col, n], stage(i, col, 1)[1]
        )

    def a_step(i, col, n):
        t_copy(i, col, n).wait_recv()
        at = pl.ds(*pieces(i)[n])
        half = stage(i, col, 1)[0]
        other, own = half_rows(1 - half, 64), half_rows(half, 64)
        asend_v[i, col, :, at] = (town_v[i, col, other, at] + trecv_v[i, col, other, at].astype(F32)).astype(BF)
        a_copy(i, col, n).start()
        aown_v[i, col, :, at] = town_v[i, col, own, at] + trecv_v[i, col, own, at].astype(F32)

    def b_copy(i, col, n):
        at = pl.ds(*pieces(i)[n])
        return remote(
            bsend_v.at[i, col, :, at], brecv_v.at[i, col, :, at], b_ssem, b_rsem.at[i, col, n], stage(i, col, 2)[1]
        )

    def b_step(i, col, n):
        a_copy(i, col, n).wait_recv()
        at = pl.ds(*pieces(i)[n])
        half = stage(i, col, 2)[0]
        other, own = half_rows(1 - half, 32), half_rows(half, 32)
        bsend_v[i, col, :, at] = (aown_v[i, col, other, at] + arecv_v[i, col, other, at].astype(F32)).astype(BF)
        b_copy(i, col, n).start()
        bown_v[i, col, :, at] = aown_v[i, col, own, at] + arecv_v[i, col, own, at].astype(F32)

    def g_copy(i, col, d):
        first, second, j, s1, pq, v, p = place(i, col)
        slot = (zl * 2 + j) * 2 + c
        to = (slot + d) % 8
        zd, jd, cd = to // 4, (to // 2) % 2, to % 2
        src = gsend_v.at[i, col, zd, pl.ds(pl.multiple_of((jd * 2 + cd) * 16, 16), 16)]
        dst = gath_v.at[i * 2 + col, pl.ds(pl.multiple_of(slot * 16, 16), 16)]
        if d == 0:
            return pltpu.make_async_copy(src, dst, g_rsem.at[i, col])
        return remote(src, dst, g_ssem, g_rsem.at[i, col], to_ring(i, (s1 * 2 + jd + col) % 4, second, cd, zd))

    def f_step(i, col):
        for n in range(len(pieces(i))):
            b_copy(i, col, n).wait_recv()
        value = bown_v[i, col] + brecv_v[i, col].astype(F32)
        tiles = [value[:, 128 * n : 128 * (n + 1)] for n in range(5)]
        lower = lax.broadcasted_iota(jnp.int32, (32, 128), 0) % 8 >= 4
        for w in range(2):
            win, rest = tiles[2 * w : 2 * w + 3], (tiles[3:] if w == 0 else tiles[:2])
            shared = jnp.where(lower, rest[0], pltpu.roll(rest[1], 28, 0))
            upper = jnp.concatenate([win[0], win[1]], axis=1).reshape(4, 8, 256)
            under = jnp.concatenate([win[2], shared], axis=1).reshape(4, 8, 256)
            gsend_v[i, col, w] = jnp.concatenate([upper, under], axis=1).reshape(64, 256).astype(BF)
        for d in (4, 5, 6, 7, 2, 3, 1, 0):
            g_copy(i, col, d).start()

    def y_copy(i, col, d):
        return remote(
            ysend_v.at[i, col, d - 1], rows_v.at[y, i, col],
            y_ssem, y_rsem.at[i], dev(zl, (y + d) % 4, x, zh, c),
        )

    def y_step(i, col):
        landed(gath_v.at[i * 2 + col], g_rsem.at[i, col])
        packed = gath_v[i * 2 + col]
        upper = dot(order_v[0], packed).astype(BF)
        under = dot(order_v[1], packed).astype(BF)
        win = [upper[:32, :128], upper[:32, 128:], under[:32, :128]]
        rest = [under[:32, 128:], under[32:, 128:]]
        right = jnp.where(zl == 0, jnp.concatenate(win + rest, axis=1), jnp.concatenate(rest + win, axis=1))
        pick_copy = dot(jnp.concatenate([upper[32:], under[32:, :128]], axis=1), pick_v[...]).astype(BF)
        lefts = [pick_copy[:, 128 * n : 128 * (n + 1)] for n in range(4)]
        for d in (2, 1, 3, 0):
            to = (y + d) % 4
            left = jnp.where(to < 2, jnp.where(to == 0, lefts[0], lefts[1]), jnp.where(to == 2, lefts[2], lefts[3]))
            if d:
                ysend_v[i, col, d - 1, :, :natural] = right
                ysend_v[i, col, d - 1, :, natural:] = left
                y_copy(i, col, d).start()
            else:
                rows_v[y, i, col, :, :natural] = right
                rows_v[y, i, col, :, natural:] = left

    def out_step(i):
        landed(rows_v.at[pl.ds(0, 3), i], y_rsem.at[i])
        both = rows_v[:, i].reshape(256, natural + 128)
        left = both[:, natural:]
        parity = lax.broadcasted_iota(jnp.int32, left.shape, 0) % 2
        zero = jnp.zeros_like(left)
        left = jnp.concatenate([jnp.where(parity == t, left, zero) for t in range(2)], axis=1)
        acc_v[...] += lax.dot_general(
            left, both[:, :natural], (((0,), (0,)), ((), ())), preferred_element_type=F32
        )

    def one_hots():
        to = lax.broadcasted_iota(jnp.int32, (64, 128), 0)
        at = lax.broadcasted_iota(jnp.int32, (64, 128), 1)
        source = (to % 32) // 4 * 16 + to % 4 + jnp.where(to < 32, 4, 0)
        for n in range(2):
            order_v[n] = jnp.where(at == source + 8 * n, 1.0, 0.0).astype(BF)
        at = lax.broadcasted_iota(jnp.int32, (384, 512), 0)
        to = lax.broadcasted_iota(jnp.int32, (384, 512), 1)
        source = (zl * 4 + to // 128) * 80 + to % 128 - zl * 256
        pick_v[...] = jnp.where((at == source) & (to % 128 < 80), 1.0, 0.0).astype(BF)
        acc_v[...] = jnp.zeros_like(acc_v)

    def drain_step():
        landed(pair_v.at[0, pl.ds(0, 7)], p_ssem.at[0])
        landed(pack_v.at[pl.ds(0, 3)], p_ssem.at[1])
        landed(half_v.at[pl.ds(0, 3)], h_ssem)
        landed(tsend_v, t_ssem)
        landed(asend_v, a_ssem)
        landed(bsend_v, b_ssem)
        landed(gath_v.at[pl.ds(0, 2 * ROUNDS - 1)], g_ssem)

    steps = {"t": t_step, "a": a_step, "b": b_step, "f": f_step, "y": y_step}
    for token in PLAN:
        name, i = token[0], int(token[1])
        if name == "h":
            half_step(i)
            half_send(i, FIRST if i in LATE else FIRST + SECOND)
        elif name == "s":
            half_send(i, SECOND)
        elif name == "o":
            out_step(i)
        elif name == "d":
            drain_step()
        elif name == "p":
            p_step()
        elif name == "w":
            w_step(i)
        elif name == "c":
            one_hots()
        elif name in "tab":
            for n in (int(token[2]),) if len(token) > 2 else range(len(pieces(i))):
                for col in range(2):
                    steps[name](i, col, n)
        else:
            for col in range(2):
                steps[name](i, col)

    for t in range(2):
        out_ref[:, t, :] = acc_v[pl.ds(128 * t, 80)]
    landed(ysend_v, y_ssem)


def constants():
    k = np.arange(4 * SUB * 40)
    dev, fun, orb = k // (SUB * 40), (k // 40) % SUB, k % 40
    a = np.arange(80)
    spread = np.stack(
        [(dev[None] == 2 * jj + a[:, None] // 40) & (orb[None] == a[:, None] % 40) for jj in range(2)]
    )
    r = np.arange(256)
    mask = ((r[:, None] // 2) % SUB) == fun[None]
    return spread.astype(np.float32), mask.astype(np.float32)


def solution(mesh):
    spread, mask = constants()

    def local(df_blocks, fno_rotation, tile_pairs):
        aux_n, orbs, nv = df_blocks.shape
        nf = fno_rotation.shape[1]
        rows = aux_n * orbs // ROUNDS
        vm = pltpu.VMEM
        dma = pltpu.SemaphoreType.DMA
        return pl.pallas_call(
            kernel,
            name="tiles",
            out_shape=pltpu.VMEM((80, 2, nf), F32),
            in_specs=[
                pl.BlockSpec(memory_space=pl.ANY),
                pl.BlockSpec(memory_space=pl.ANY),
                pl.BlockSpec(memory_space=pltpu.SMEM),
                pl.BlockSpec(memory_space=pl.ANY),
                pl.BlockSpec(memory_space=pl.ANY),
            ],
            out_specs=pl.BlockSpec(memory_space=pltpu.VMEM),
            scratch_shapes=[
                vm((2, 80, 4 * SUB * 40), BF),
                vm((256, 4 * SUB * 40), BF),
                vm((ROUNDS, rows, nv), BF),
                vm((nv, nf), BF),
                vm((ROUNDS, rows, nf), BF),
                vm((ROUNDS, 2, rows // 2, nf), BF),
                vm((4, 8, 8, 128), jnp.int32),
                vm((4, 8, 128), jnp.int32),
                vm((256, nf), BF),
                vm((4, 256, 4 * SUB * 40), BF),
                vm((ROUNDS, 2, 128, nf), BF),
                vm((ROUNDS, 2, 128, nf), F32),
                vm((ROUNDS, 2, 128, nf), BF),
                vm((ROUNDS, 2, 64, nf), BF),
                vm((ROUNDS, 2, 64, nf), F32),
                vm((ROUNDS, 2, 64, nf), BF),
                vm((ROUNDS, 2, 32, nf), BF),
                vm((ROUNDS, 2, 32, nf), F32),
                vm((ROUNDS, 2, 32, nf), BF),
                vm((ROUNDS, 2, 2, 64, 256), BF),
                vm((ROUNDS * 2, 128, 256), BF),
                vm((2, 64, 128), BF),
                vm((384, 512), BF),
                vm((4, ROUNDS, 2, 32, nf + 128), BF),
                vm((ROUNDS, 2, 3, 32, nf + 128), BF),
                vm((256, nf), F32),
                dma((2,)),
                dma((ROUNDS,)),
                dma(()),
                dma((2,)), dma((2,)),
                dma(()), dma((ROUNDS, 2)),
                dma(()), dma((ROUNDS, 2, 3)),
                dma(()), dma((ROUNDS, 2, 3)),
                dma(()), dma((ROUNDS, 2, 3)),
                dma(()), dma((ROUNDS, 2)),
                dma(()), dma((ROUNDS,)),
            ],
            compiler_params=pltpu.CompilerParams(
                collective_id=0, has_side_effects=True, vmem_limit_bytes=59392 * 2**10
            ),
        )(
            df_blocks.reshape(aux_n * orbs, nv),
            fno_rotation,
            tile_pairs,
            jnp.asarray(spread, BF),
            jnp.asarray(mask, BF),
        )

    placed = (P("aux", "virt", None), P(), P("virt", None))
    return jax.shard_map(local, mesh=mesh, in_specs=placed, out_specs=P("aux", "virt", None), check_vma=False)
```

```python
import jax
import jax.numpy as jnp
import numpy as np
from jax import lax
from jax.experimental import pallas as pl
from jax.experimental.pallas import tpu as pltpu
from jax.sharding import PartitionSpec as P

MESH = pl.DeviceIdType.MESH
BF = jnp.bfloat16
F32 = jnp.float32

ROUNDS = 4
Z_ROUNDS = (1,)
FIRST, SECOND = (2, 1, 0), (3,)
LATE = (2,)
SPLIT = (0, 1, 2, 3)
PLAN = (
    "h3", "p0", "h1", "w0", "t0", "h2", "t3", "a0", "s2", "b0", "a3", "w1", "t2", "c0", "f0", "t1", "b3",
    "a2", "f3", "y0", "a1", "b2", "b1", "y3", "f2", "f1", "o0", "y2", "o3", "y1", "o2", "d0", "o1",
)
SUB = 2


def pieces(i):
    return ((0, 384), (384, 256)) if i in SPLIT else ((0, 640),)


def dot(a, b):
    return jnp.dot(a, b, preferred_element_type=F32)


def dot_nt(a, b):
    return lax.dot_general(a, b, (((1,), (1,)), ((), ())), preferred_element_type=F32)


def kernel(
    df_ref, rot_ref, pairs_ref, spread_ref, mask_ref, out_ref,
    spread_v, mask_v, df_v, rot_v, half_v, quad_v, pair_v, pack_v, hot_v, w_v, tsend_v, town_v, trecv_v,
    asend_v, aown_v, arecv_v, bsend_v, bown_v, brecv_v, gsend_v, gath_v, order_v, pick_v, rows_v, ysend_v, acc_v,
    c_sem, df_sem, rot_sem, p_ssem, p_rsem, h_ssem, h_rsem, t_ssem, t_rsem,
    a_ssem, a_rsem, b_ssem, b_rsem, g_ssem, g_rsem, y_ssem, y_rsem,
):
    natural = rot_v.shape[1]
    aux = lax.axis_index("aux")
    virt = lax.axis_index("virt")
    zl, y = aux // 4, aux % 4
    x, zh, c = virt // 8, (virt // 2) % 4, virt % 2
    hrows = half_v.shape[1] // 8
    rrows = half_v.shape[1]

    def dev(zl_, y_, x_, zh_, c_):
        return (zl_ * 4 + y_, (x_ * 4 + zh_) * 2 + c_)

    def remote(src, dst, ssem, rsem, device):
        return pltpu.make_async_remote_copy(
            src_ref=src, dst_ref=dst, send_sem=ssem, recv_sem=rsem, device_id=device, device_id_type=MESH
        )

    def landed(ref, sem):
        pltpu.make_async_copy(ref, ref, sem).wait()

    def df_copy(i):
        return pltpu.make_async_copy(df_ref.at[pl.ds(i * rrows, rrows)], df_v.at[i], df_sem.at[i])

    first_copies = []
    for n in range(4):
        at = pl.ds(n * rot_v.shape[0] // 4, rot_v.shape[0] // 4)
        first_copies.append(pltpu.make_async_copy(rot_ref.at[at], rot_v.at[at], rot_sem))
        at = pl.ds(n * rrows // 4, rrows // 4)
        first_copies.append(pltpu.make_async_copy(df_ref.at[at], df_v.at[0, at], df_sem.at[0]))
    for copy in first_copies:
        copy.start()

    xr, xl = (x + 1) % 4, (x + 3) % 4
    xo = (x + 2) % 4
    peers = [dev(zl, y, x, zh, 1 - c)]
    peers += [dev(zl, y, xx, zh, cc) for xx in (xr, xl, xo) for cc in range(2)]
    peers += [dev(zl, y, x, (zh + d) % 4, c) for d in range(1, 4)]
    peers += [dev(zl, y, x, (zh + d) % 4, 1 - c) for d in (1, 3)]
    peers += [dev(1 - zl, y, x, (zh + d) % 4, cc) for d in (1, 3) for cc in range(2)]
    peers += [dev(1 - zl, y, xx, zh, cc) for xx in (x, xr, xl) for cc in range(2)]
    peers += [dev(zl, (y + d) % 4, x, zh, c) for d in range(1, 4)]
    barrier = pltpu.get_barrier_semaphore()
    for peer in peers:
        pl.semaphore_signal(barrier, inc=1, device_id=peer, device_id_type=MESH)

    row = lax.broadcasted_iota(jnp.int32, (8, 128), 0)
    tile = row % 2
    side = row // 4
    mine = jnp.where(
        side == 0,
        jnp.where(tile == 0, pairs_ref[0, 0], pairs_ref[1, 0]),
        jnp.where(tile == 0, pairs_ref[0, 1], pairs_ref[1, 1]),
    )
    pair_v[zh, x * 2 + c] = mine

    def to_ring(i, first, second, core, zl_=zl):
        return dev(zl_, y, second, first, core) if i in Z_ROUNDS else dev(zl_, y, first, second, core)

    def place(i, col):
        first, second = (zh, x) if i in Z_ROUNDS else (x, zh)
        u, v = (first + 4 - col) % 4, (second + 4 - col) % 4
        p = (v + 3) % 4
        return first, second, u % 2, u // 2, (u % 2 + u // 2) % 2, v, p

    def stage(i, col, n):
        first, second, j, s1, pq, v, p = place(i, col)
        n = (n + 1) % 3 if i in Z_ROUNDS else n
        if n == 0:
            return s1, to_ring(i, (first + jnp.where(j == 1, 1, 3)) % 4, second, c)
        if n == 1:
            return p // 2, to_ring(i, first, (v + 1 - 2 * (v % 2) + col) % 4, c)
        return p % 2, to_ring(i, first, (p + 2 - 2 * (p % 2) + col) % 4, c)

    def h_copy(i, col, d):
        first, second, j, s1, pq, v, p = place(i, col)
        q, cd = (pq + d // 2) % 2, (c + d % 2) % 2
        fd = (s1 * 2 + (q + s1) % 2 + col) % 4
        src = half_v.at[i, pl.ds(pl.multiple_of(col * 4 * hrows + (q * 2 + cd) * hrows, 16), hrows)]
        dst = quad_v.at[i, col, pl.ds(pl.multiple_of((j * 2 + c) * hrows, 16), hrows)]
        if d == 0:
            return pltpu.make_async_copy(src, dst, h_rsem.at[i, col])
        return remote(src, dst, h_ssem, h_rsem.at[i, col], to_ring(i, fd, second, cd))

    def half_step(i):
        landed(df_v.at[i], df_sem.at[i])
        for at in (pl.ds(0, rrows // 2), pl.ds(rrows // 2, rrows // 2)):
            for lo in range(0, natural, 256):
                to = pl.ds(lo, min(256, natural - lo))
                half_v[i, at, to] = dot(df_v[i, at], rot_v[:, to]).astype(BF)

    def half_send(i, ds=(2, 3, 1, 0)):
        for d in ds:
            for col in range(2):
                h_copy(i, col, d).start()

    def p_first(n):
        ref = pair_v.at[zh, x * 2 + c]
        xx = (x, xr, xr, xl, xl, xo, xo)[n]
        cc = (1 - c, c, 1 - c, c, 1 - c, c, 1 - c)[n]
        return remote(ref, ref, p_ssem.at[0], p_rsem.at[0], dev(zl, y, xx, zh, cc))

    def p_second(d):
        ref = pack_v.at[zh]
        return remote(ref, ref, p_ssem.at[1], p_rsem.at[1], dev(zl, y, x, (zh + d) % 4, c))

    def p_step():
        landed(pair_v.at[0, pl.ds(0, 7)], p_rsem.at[0])
        lane = lax.broadcasted_iota(jnp.int32, (8, 128), 1)
        packed = pair_v[zh, 0]
        for k in range(1, 8):
            packed = jnp.where(lane >= 16 * k, pair_v[zh, k], packed)
        pack_v[zh] = packed
        for d in (2, 1, 3):
            p_second(d).start()

    landed(rot_v, rot_sem)
    const_copies = (
        pltpu.make_async_copy(spread_ref, spread_v, c_sem.at[0]),
        pltpu.make_async_copy(mask_ref, mask_v, c_sem.at[1]),
    )
    half_step(0)
    for i in (3, 1, 2):
        df_copy(i).start()
    for copy in const_copies:
        copy.start()
    pl.semaphore_wait(barrier, len(peers))
    for n in range(7):
        p_first(n).start()
    half_send(0)

    def w_step(i):
        if i == 0:
            landed(pack_v.at[pl.ds(0, 3)], p_rsem.at[1])
            for copy in const_copies:
                copy.wait()
        blocks = [
            [jnp.broadcast_to(pack_v[z][:, 16 * k : 16 * k + 1], (8, 128)) for k in range(8)] for z in range(4)
        ]
        two = range(2)
        for col in range(2):
            first, second, j, s1, pq, v, p = place(i, col)
            if i in Z_ROUNDS:
                order = [
                    ((2 * h + jj + col) % 4, (2 * s2 + s3 + 1 + col) % 4, cc)
                    for s2 in two for s3 in two for h in two for jj in two for cc in two
                ]
            else:
                order = [
                    ((2 * s2 + s3 + 1 + col) % 4, (2 * h + jj + col) % 4, cc)
                    for h in two for s2 in two for s3 in two for jj in two for cc in two
                ]
            wanted = jnp.concatenate([blocks[z][xx * 2 + cc] for z, xx, cc in order], axis=0)
            at = lax.broadcasted_iota(jnp.int32, wanted.shape, 1)
            for n in range(natural // 128):
                hot_v[:, n * 128 : (n + 1) * 128] = jnp.where(wanted == at + n * 128, 1.0, 0.0).astype(BF)
            rows = []
            for jj in two:
                fs = (s1 * 2 + jj + col) % 4
                chip = x * 4 + fs if i in Z_ROUNDS else fs * 4 + zh
                rows.append(rot_v[pl.ds(pl.multiple_of(chip * 80, 16), 80)])
            sel = dot_nt(hot_v[...], jnp.concatenate(rows, axis=0)).astype(BF)
            total = dot(sel, spread_v[...].reshape(160, 4 * SUB * 40))
            w_v[kind(i) * 2 + col] = (total * mask_v[...].astype(F32)).astype(BF)

    def kind(i):
        return 1 if i in Z_ROUNDS else 0

    def half_rows(half, size):
        return pl.ds(pl.multiple_of(half * size, size), size)

    def t_copy(i, col, n):
        at = pl.ds(*pieces(i)[n])
        return remote(
            tsend_v.at[i, col, :, at], trecv_v.at[i, col, :, at], t_ssem, t_rsem.at[i, col, n], stage(i, col, 0)[1]
        )

    def t_step(i, col, n):
        if n == 0:
            landed(quad_v.at[i, col], h_rsem.at[i, col])
        at = pl.ds(*pieces(i)[n])
        half = stage(i, col, 0)[0]
        w = w_v.at[kind(i) * 2 + col]
        tsend_v[i, col, :, at] = dot(w[half_rows(1 - half, 128)], quad_v[i, col, :, at]).astype(BF)
        t_copy(i, col, n).start()

    def t_own_step(i, col):
        w = w_v.at[kind(i) * 2 + col]
        town_v[i, col] = dot(w[half_rows(stage(i, col, 0)[0], 128)], quad_v[i, col])

    def a_copy(i, col, n):
        at = pl.ds(*pieces(i)[n])
        return remote(
            asend_v.at[i, col, :, at], arecv_v.at[i, col, :, at], a_ssem, a_rsem.at[i, col, n], stage(i, col, 1)[1]
        )

    def a_step(i, col, n):
        t_copy(i, col, n).wait_recv()
        at = pl.ds(*pieces(i)[n])
        half = stage(i, col, 1)[0]
        other, own = half_rows(1 - half, 64), half_rows(half, 64)
        asend_v[i, col, :, at] = (town_v[i, col, other, at] + trecv_v[i, col, other, at].astype(F32)).astype(BF)
        a_copy(i, col, n).start()
        aown_v[i, col, :, at] = town_v[i, col, own, at] + trecv_v[i, col, own, at].astype(F32)

    def b_copy(i, col, n):
        at = pl.ds(*pieces(i)[n])
        return remote(
            bsend_v.at[i, col, :, at], brecv_v.at[i, col, :, at], b_ssem, b_rsem.at[i, col, n], stage(i, col, 2)[1]
        )

    def b_step(i, col, n):
        a_copy(i, col, n).wait_recv()
        at = pl.ds(*pieces(i)[n])
        half = stage(i, col, 2)[0]
        other, own = half_rows(1 - half, 32), half_rows(half, 32)
        bsend_v[i, col, :, at] = (aown_v[i, col, other, at] + arecv_v[i, col, other, at].astype(F32)).astype(BF)
        b_copy(i, col, n).start()
        bown_v[i, col, :, at] = aown_v[i, col, own, at] + arecv_v[i, col, own, at].astype(F32)

    def g_copy(i, col, d):
        first, second, j, s1, pq, v, p = place(i, col)
        slot = (zl * 2 + j) * 2 + c
        zd, jd, cd = (zl + d // 4) % 2, (j + d // 2) % 2, (c + d) % 2
        src = gsend_v.at[i, col, zd, pl.ds(pl.multiple_of((jd * 2 + cd) * 16, 16), 16)]
        dst = gath_v.at[i * 2 + col, pl.ds(pl.multiple_of(slot * 16, 16), 16)]
        if d == 0:
            return pltpu.make_async_copy(src, dst, g_rsem.at[i, col])
        return remote(src, dst, g_ssem, g_rsem.at[i, col], to_ring(i, (s1 * 2 + jd + col) % 4, second, cd, zd))

    def f_step(i, col):
        for n in range(len(pieces(i))):
            b_copy(i, col, n).wait_recv()
        value = bown_v[i, col] + brecv_v[i, col].astype(F32)
        tiles = [value[:, 128 * n : 128 * (n + 1)] for n in range(5)]
        lower = lax.broadcasted_iota(jnp.int32, (32, 128), 0) % 8 >= 4
        for w in range(2):
            win, rest = tiles[2 * w : 2 * w + 3], (tiles[3:] if w == 0 else tiles[:2])
            shared = jnp.where(lower, rest[0], pltpu.roll(rest[1], 28, 0))
            upper = jnp.concatenate([win[0], win[1]], axis=1).reshape(4, 8, 256)
            under = jnp.concatenate([win[2], shared], axis=1).reshape(4, 8, 256)
            gsend_v[i, col, w] = jnp.concatenate([upper, under], axis=1).reshape(64, 256).astype(BF)
        for d in (7, 6, 5, 4, 3, 2, 1, 0):
            g_copy(i, col, d).start()

    def y_copy(i, col, d):
        return remote(
            ysend_v.at[i, col, d - 1], rows_v.at[y, i, col],
            y_ssem, y_rsem.at[i], dev(zl, (y + d) % 4, x, zh, c),
        )

    def y_step(i, col):
        landed(gath_v.at[i * 2 + col], g_rsem.at[i, col])
        packed = gath_v[i * 2 + col]
        upper = dot(order_v[0], packed).astype(BF)
        under = dot(order_v[1], packed).astype(BF)
        win = [upper[:32, :128], upper[:32, 128:], under[:32, :128]]
        rest = [under[:32, 128:], under[32:, 128:]]
        right = jnp.where(zl == 0, jnp.concatenate(win + rest, axis=1), jnp.concatenate(rest + win, axis=1))
        pick_copy = dot(jnp.concatenate([upper[32:], under[32:, :128]], axis=1), pick_v[...]).astype(BF)
        lefts = [pick_copy[:, 128 * n : 128 * (n + 1)] for n in range(4)]
        for d in (2, 1, 3, 0):
            to = (y + d) % 4
            left = jnp.where(to < 2, jnp.where(to == 0, lefts[0], lefts[1]), jnp.where(to == 2, lefts[2], lefts[3]))
            if d:
                ysend_v[i, col, d - 1, :, :natural] = right
                ysend_v[i, col, d - 1, :, natural:] = left
                y_copy(i, col, d).start()
            else:
                rows_v[y, i, col, :, :natural] = right
                rows_v[y, i, col, :, natural:] = left

    def out_step(i):
        landed(rows_v.at[pl.ds(0, 3), i], y_rsem.at[i])
        both = rows_v[:, i].reshape(256, natural + 128)
        left = both[:, natural:]
        parity = lax.broadcasted_iota(jnp.int32, left.shape, 0) % 2
        zero = jnp.zeros_like(left)
        left = jnp.concatenate([jnp.where(parity == t, left, zero) for t in range(2)], axis=1)
        acc_v[...] += lax.dot_general(
            left, both[:, :natural], (((0,), (0,)), ((), ())), preferred_element_type=F32
        )

    def one_hots():
        to = lax.broadcasted_iota(jnp.int32, (64, 128), 0)
        at = lax.broadcasted_iota(jnp.int32, (64, 128), 1)
        source = (to % 32) // 4 * 16 + to % 4 + jnp.where(to < 32, 4, 0)
        for n in range(2):
            order_v[n] = jnp.where(at == source + 8 * n, 1.0, 0.0).astype(BF)
        at = lax.broadcasted_iota(jnp.int32, (384, 512), 0)
        to = lax.broadcasted_iota(jnp.int32, (384, 512), 1)
        source = (zl * 4 + to // 128) * 80 + to % 128 - zl * 256
        pick_v[...] = jnp.where((at == source) & (to % 128 < 80), 1.0, 0.0).astype(BF)
        acc_v[...] = jnp.zeros_like(acc_v)

    def drain_step():
        landed(pair_v.at[0, pl.ds(0, 7)], p_ssem.at[0])
        landed(pack_v.at[pl.ds(0, 3)], p_ssem.at[1])
        landed(half_v.at[pl.ds(0, 3)], h_ssem)
        landed(tsend_v, t_ssem)
        landed(asend_v, a_ssem)
        landed(bsend_v, b_ssem)
        landed(gath_v.at[pl.ds(0, 2 * ROUNDS - 1)], g_ssem)

    steps = {"t": t_step, "a": a_step, "b": b_step, "f": f_step, "y": y_step}
    for token in PLAN:
        name, i = token[0], int(token[1])
        if name == "h":
            half_step(i)
            half_send(i, FIRST if i in LATE else FIRST + SECOND)
        elif name == "s":
            half_send(i, SECOND)
        elif name == "o":
            out_step(i)
        elif name == "d":
            drain_step()
        elif name == "p":
            p_step()
        elif name == "w":
            w_step(i)
        elif name == "c":
            one_hots()
        elif name in "tab":
            for n in (int(token[2]),) if len(token) > 2 else range(len(pieces(i))):
                for col in range(2):
                    steps[name](i, col, n)
            if name == "t":
                for col in range(2):
                    t_own_step(i, col)
        else:
            for col in range(2):
                steps[name](i, col)

    for t in range(2):
        out_ref[:, t, :] = acc_v[pl.ds(128 * t, 80)]
    landed(ysend_v, y_ssem)


def constants():
    k = np.arange(4 * SUB * 40)
    dev, fun, orb = k // (SUB * 40), (k // 40) % SUB, k % 40
    a = np.arange(80)
    spread = np.stack(
        [(dev[None] == 2 * jj + a[:, None] // 40) & (orb[None] == a[:, None] % 40) for jj in range(2)]
    )
    r = np.arange(256)
    mask = ((r[:, None] // 2) % SUB) == fun[None]
    return spread.astype(np.float32), mask.astype(np.float32)


def solution(mesh):
    spread, mask = constants()

    def local(df_blocks, fno_rotation, tile_pairs):
        aux_n, orbs, nv = df_blocks.shape
        nf = fno_rotation.shape[1]
        rows = aux_n * orbs // ROUNDS
        vm = pltpu.VMEM
        dma = pltpu.SemaphoreType.DMA
        return pl.pallas_call(
            kernel,
            name="tiles",
            out_shape=pltpu.VMEM((80, 2, nf), F32),
            in_specs=[
                pl.BlockSpec(memory_space=pl.ANY),
                pl.BlockSpec(memory_space=pl.ANY),
                pl.BlockSpec(memory_space=pltpu.SMEM),
                pl.BlockSpec(memory_space=pl.ANY),
                pl.BlockSpec(memory_space=pl.ANY),
            ],
            out_specs=pl.BlockSpec(memory_space=pltpu.VMEM),
            scratch_shapes=[
                vm((2, 80, 4 * SUB * 40), BF),
                vm((256, 4 * SUB * 40), BF),
                vm((ROUNDS, rows, nv), BF),
                vm((nv, nf), BF),
                vm((ROUNDS, rows, nf), BF),
                vm((ROUNDS, 2, rows // 2, nf), BF),
                vm((4, 8, 8, 128), jnp.int32),
                vm((4, 8, 128), jnp.int32),
                vm((256, nf), BF),
                vm((4, 256, 4 * SUB * 40), BF),
                vm((ROUNDS, 2, 128, nf), BF),
                vm((ROUNDS, 2, 128, nf), F32),
                vm((ROUNDS, 2, 128, nf), BF),
                vm((ROUNDS, 2, 64, nf), BF),
                vm((ROUNDS, 2, 64, nf), F32),
                vm((ROUNDS, 2, 64, nf), BF),
                vm((ROUNDS, 2, 32, nf), BF),
                vm((ROUNDS, 2, 32, nf), F32),
                vm((ROUNDS, 2, 32, nf), BF),
                vm((ROUNDS, 2, 2, 64, 256), BF),
                vm((ROUNDS * 2, 128, 256), BF),
                vm((2, 64, 128), BF),
                vm((384, 512), BF),
                vm((4, ROUNDS, 2, 32, nf + 128), BF),
                vm((ROUNDS, 2, 3, 32, nf + 128), BF),
                vm((256, nf), F32),
                dma((2,)),
                dma((ROUNDS,)),
                dma(()),
                dma((2,)), dma((2,)),
                dma(()), dma((ROUNDS, 2)),
                dma(()), dma((ROUNDS, 2, 3)),
                dma(()), dma((ROUNDS, 2, 3)),
                dma(()), dma((ROUNDS, 2, 3)),
                dma(()), dma((ROUNDS, 2)),
                dma(()), dma((ROUNDS,)),
            ],
            compiler_params=pltpu.CompilerParams(
                collective_id=0, has_side_effects=True, vmem_limit_bytes=59392 * 2**10
            ),
        )(
            df_blocks.reshape(aux_n * orbs, nv),
            fno_rotation,
            tile_pairs,
            jnp.asarray(spread, BF),
            jnp.asarray(mask, BF),
        )

    placed = (P("aux", "virt", None), P(), P("virt", None))
    return jax.shard_map(local, mesh=mesh, in_specs=placed, out_specs=P("aux", "virt", None), check_vma=False)
```

```python
import jax
import jax.numpy as jnp
import numpy as np
from jax import lax
from jax.experimental import pallas as pl
from jax.experimental.pallas import tpu as pltpu
from jax.sharding import PartitionSpec as P

MESH = pl.DeviceIdType.MESH
BF = jnp.bfloat16
F32 = jnp.float32

ROUNDS = 4
Z_ROUNDS = (1,)
FIRST, SECOND = (2, 1, 0), (3,)
LATE = (2,)
SPLIT = (0, 1, 2, 3)
PLAN = (
    "h3", "p0", "h1", "w0", "t0", "h2", "t3", "a0", "s2", "b0", "a3", "w1", "t2", "c0", "f0", "t1", "b3",
    "a2", "f3", "y0", "a1", "b2", "b1", "y3", "f2", "f1", "o0", "y2", "o3", "y1", "o2", "d0", "o1",
)
SUB = 2


def pieces(i):
    return ((0, 384), (384, 256)) if i in SPLIT else ((0, 640),)


def dot(a, b):
    return jnp.dot(a, b, preferred_element_type=F32)


def dot_nt(a, b):
    return lax.dot_general(a, b, (((1,), (1,)), ((), ())), preferred_element_type=F32)


def kernel(
    df_ref, rot_ref, pairs_ref, spread_ref, mask_ref, out_ref,
    spread_v, mask_v, df_v, rot_v, half_v, quad_v, pair_v, pack_v, hot_v, w_v, tsend_v, town_v, trecv_v,
    asend_v, aown_v, arecv_v, bsend_v, bown_v, brecv_v, gsend_v, gath_v, order_v, pick_v, rows_v, ysend_v, acc_v,
    c_sem, df_sem, rot_sem, p_ssem, p_rsem, h_ssem, h_rsem, t_ssem, t_rsem,
    a_ssem, a_rsem, b_ssem, b_rsem, g_ssem, g_rsem, y_ssem, y_rsem,
):
    natural = rot_v.shape[1]
    aux = lax.axis_index("aux")
    virt = lax.axis_index("virt")
    zl, y = aux // 4, aux % 4
    x, zh, c = virt // 8, (virt // 2) % 4, virt % 2
    hrows = half_v.shape[1] // 8
    rrows = half_v.shape[1]

    def dev(zl_, y_, x_, zh_, c_):
        return (zl_ * 4 + y_, (x_ * 4 + zh_) * 2 + c_)

    def remote(src, dst, ssem, rsem, device):
        return pltpu.make_async_remote_copy(
            src_ref=src, dst_ref=dst, send_sem=ssem, recv_sem=rsem, device_id=device, device_id_type=MESH
        )

    def landed(ref, sem):
        pltpu.make_async_copy(ref, ref, sem).wait()

    def df_copy(i):
        return pltpu.make_async_copy(df_ref.at[pl.ds(i * rrows, rrows)], df_v.at[i], df_sem.at[i])

    first_copies = []
    for n in range(4):
        at = pl.ds(n * rot_v.shape[0] // 4, rot_v.shape[0] // 4)
        first_copies.append(pltpu.make_async_copy(rot_ref.at[at], rot_v.at[at], rot_sem))
        at = pl.ds(n * rrows // 4, rrows // 4)
        first_copies.append(pltpu.make_async_copy(df_ref.at[at], df_v.at[0, at], df_sem.at[0]))
    for copy in first_copies:
        copy.start()

    xr, xl = (x + 1) % 4, (x + 3) % 4
    xo = (x + 2) % 4
    peers = [dev(zl, y, x, zh, 1 - c)]
    peers += [dev(zl, y, xx, zh, cc) for xx in (xr, xl, xo) for cc in range(2)]
    peers += [dev(zl, y, x, (zh + d) % 4, c) for d in range(1, 4)]
    peers += [dev(zl, y, x, (zh + d) % 4, 1 - c) for d in (1, 3)]
    peers += [dev(1 - zl, y, x, (zh + d) % 4, cc) for d in (1, 3) for cc in range(2)]
    peers += [dev(1 - zl, y, xx, zh, cc) for xx in (x, xr, xl) for cc in range(2)]
    peers += [dev(zl, (y + d) % 4, x, zh, c) for d in range(1, 4)]
    barrier = pltpu.get_barrier_semaphore()
    for peer in peers:
        pl.semaphore_signal(barrier, inc=1, device_id=peer, device_id_type=MESH)

    row = lax.broadcasted_iota(jnp.int32, (8, 128), 0)
    tile = row % 2
    side = row // 4
    mine = jnp.where(
        side == 0,
        jnp.where(tile == 0, pairs_ref[0, 0], pairs_ref[1, 0]),
        jnp.where(tile == 0, pairs_ref[0, 1], pairs_ref[1, 1]),
    )
    pair_v[zh, x * 2 + c] = mine

    def to_ring(i, first, second, core, zl_=zl):
        return dev(zl_, y, second, first, core) if i in Z_ROUNDS else dev(zl_, y, first, second, core)

    def place(i, col):
        first, second = (zh, x) if i in Z_ROUNDS else (x, zh)
        u, v = (first + 4 - col) % 4, (second + 4 - col) % 4
        p = (v + 3) % 4
        return first, second, u % 2, u // 2, (u % 2 + u // 2) % 2, v, p

    def stage(i, col, n):
        first, second, j, s1, pq, v, p = place(i, col)
        n = (n + 1) % 3 if i in Z_ROUNDS else n
        if n == 0:
            return s1, to_ring(i, (first + jnp.where(j == 1, 1, 3)) % 4, second, c)
        if n == 1:
            return p // 2, to_ring(i, first, (v + 1 - 2 * (v % 2) + col) % 4, c)
        return p % 2, to_ring(i, first, (p + 2 - 2 * (p % 2) + col) % 4, c)

    def h_copy(i, col, d):
        first, second, j, s1, pq, v, p = place(i, col)
        q, cd = (pq + d // 2) % 2, (c + d % 2) % 2
        fd = (s1 * 2 + (q + s1) % 2 + col) % 4
        src = half_v.at[i, pl.ds(pl.multiple_of(col * 4 * hrows + (q * 2 + cd) * hrows, 16), hrows)]
        dst = quad_v.at[i, col, pl.ds(pl.multiple_of((j * 2 + c) * hrows, 16), hrows)]
        if d == 0:
            return pltpu.make_async_copy(src, dst, h_rsem.at[i, col])
        return remote(src, dst, h_ssem, h_rsem.at[i, col], to_ring(i, fd, second, cd))

    def half_step(i):
        landed(df_v.at[i], df_sem.at[i])
        for at in (pl.ds(0, rrows // 2), pl.ds(rrows // 2, rrows // 2)):
            for lo in range(0, natural, 256):
                to = pl.ds(lo, min(256, natural - lo))
                half_v[i, at, to] = dot(df_v[i, at], rot_v[:, to]).astype(BF)

    def half_send(i, ds=(2, 3, 1, 0)):
        for d in ds:
            for col in range(2):
                h_copy(i, col, d).start()

    def p_first(n):
        ref = pair_v.at[zh, x * 2 + c]
        xx = (x, xr, xr, xl, xl, xo, xo)[n]
        cc = (1 - c, c, 1 - c, c, 1 - c, c, 1 - c)[n]
        return remote(ref, ref, p_ssem.at[0], p_rsem.at[0], dev(zl, y, xx, zh, cc))

    def p_second(d):
        ref = pack_v.at[zh]
        return remote(ref, ref, p_ssem.at[1], p_rsem.at[1], dev(zl, y, x, (zh + d) % 4, c))

    def p_step():
        landed(pair_v.at[0, pl.ds(0, 7)], p_rsem.at[0])
        lane = lax.broadcasted_iota(jnp.int32, (8, 128), 1)
        packed = pair_v[zh, 0]
        for k in range(1, 8):
            packed = jnp.where(lane >= 16 * k, pair_v[zh, k], packed)
        pack_v[zh] = packed
        for d in (2, 1, 3):
            p_second(d).start()

    landed(rot_v, rot_sem)
    const_copies = (
        pltpu.make_async_copy(spread_ref, spread_v, c_sem.at[0]),
        pltpu.make_async_copy(mask_ref, mask_v, c_sem.at[1]),
    )
    half_step(0)
    for i in (3, 1, 2):
        df_copy(i).start()
    for copy in const_copies:
        copy.start()
    pl.semaphore_wait(barrier, len(peers))
    for n in range(7):
        p_first(n).start()
    half_send(0)

    def w_step(i):
        if i == 0:
            landed(pack_v.at[pl.ds(0, 3)], p_rsem.at[1])
            for copy in const_copies:
                copy.wait()
        blocks = [
            [jnp.broadcast_to(pack_v[z][:, 16 * k : 16 * k + 1], (8, 128)) for k in range(8)] for z in range(4)
        ]
        two = range(2)
        for col in range(2):
            first, second, j, s1, pq, v, p = place(i, col)
            if i in Z_ROUNDS:
                order = [
                    ((2 * h + jj + col) % 4, (2 * s2 + s3 + 1 + col) % 4, cc)
                    for s2 in two for s3 in two for h in two for jj in two for cc in two
                ]
            else:
                order = [
                    ((2 * s2 + s3 + 1 + col) % 4, (2 * h + jj + col) % 4, cc)
                    for h in two for s2 in two for s3 in two for jj in two for cc in two
                ]
            wanted = jnp.concatenate([blocks[z][xx * 2 + cc] for z, xx, cc in order], axis=0)
            at = lax.broadcasted_iota(jnp.int32, wanted.shape, 1)
            for n in range(natural // 128):
                hot_v[:, n * 128 : (n + 1) * 128] = jnp.where(wanted == at + n * 128, 1.0, 0.0).astype(BF)
            rows = []
            for jj in two:
                fs = (s1 * 2 + jj + col) % 4
                chip = x * 4 + fs if i in Z_ROUNDS else fs * 4 + zh
                rows.append(rot_v[pl.ds(pl.multiple_of(chip * 80, 16), 80)])
            sel = dot_nt(hot_v[...], jnp.concatenate(rows, axis=0)).astype(BF)
            total = dot(sel, spread_v[...].reshape(160, 4 * SUB * 40))
            w_v[kind(i) * 2 + col] = (total * mask_v[...].astype(F32)).astype(BF)

    def kind(i):
        return 1 if i in Z_ROUNDS else 0

    def half_rows(half, size):
        return pl.ds(pl.multiple_of(half * size, size), size)

    def t_copy(i, col, n):
        at = pl.ds(*pieces(i)[n])
        return remote(
            tsend_v.at[i, col, :, at], trecv_v.at[i, col, :, at], t_ssem, t_rsem.at[i, col, n], stage(i, col, 0)[1]
        )

    def t_step(i, col, n):
        if n == 0:
            landed(quad_v.at[i, col], h_rsem.at[i, col])
        at = pl.ds(*pieces(i)[n])
        half = stage(i, col, 0)[0]
        w = w_v.at[kind(i) * 2 + col]
        tsend_v[i, col, :, at] = dot(w[half_rows(1 - half, 128)], quad_v[i, col, :, at]).astype(BF)
        t_copy(i, col, n).start()

    def t_own_step(i, col):
        w = w_v.at[kind(i) * 2 + col]
        town_v[i, col] = dot(w[half_rows(stage(i, col, 0)[0], 128)], quad_v[i, col])

    def a_copy(i, col, n):
        at = pl.ds(*pieces(i)[n])
        return remote(
            asend_v.at[i, col, :, at], arecv_v.at[i, col, :, at], a_ssem, a_rsem.at[i, col, n], stage(i, col, 1)[1]
        )

    def a_step(i, col, n):
        t_copy(i, col, n).wait_recv()
        at = pl.ds(*pieces(i)[n])
        half = stage(i, col, 1)[0]
        other, own = half_rows(1 - half, 64), half_rows(half, 64)
        asend_v[i, col, :, at] = (town_v[i, col, other, at] + trecv_v[i, col, other, at].astype(F32)).astype(BF)
        a_copy(i, col, n).start()
        aown_v[i, col, :, at] = town_v[i, col, own, at] + trecv_v[i, col, own, at].astype(F32)

    def b_copy(i, col, n):
        at = pl.ds(*pieces(i)[n])
        return remote(
            bsend_v.at[i, col, :, at], brecv_v.at[i, col, :, at], b_ssem, b_rsem.at[i, col, n], stage(i, col, 2)[1]
        )

    def b_step(i, col, n):
        a_copy(i, col, n).wait_recv()
        at = pl.ds(*pieces(i)[n])
        half = stage(i, col, 2)[0]
        other, own = half_rows(1 - half, 32), half_rows(half, 32)
        bsend_v[i, col, :, at] = (aown_v[i, col, other, at] + arecv_v[i, col, other, at].astype(F32)).astype(BF)
        b_copy(i, col, n).start()
        bown_v[i, col, :, at] = aown_v[i, col, own, at] + arecv_v[i, col, own, at].astype(F32)

    def g_copy(i, col, d):
        first, second, j, s1, pq, v, p = place(i, col)
        slot = (zl * 2 + j) * 2 + c
        zd, jd, cd = (zl + d // 4) % 2, (j + d // 2) % 2, (c + d) % 2
        src = gsend_v.at[i, col, zd, pl.ds(pl.multiple_of((jd * 2 + cd) * 16, 16), 16)]
        dst = gath_v.at[i * 2 + col, pl.ds(pl.multiple_of(slot * 16, 16), 16)]
        if d == 0:
            return pltpu.make_async_copy(src, dst, g_rsem.at[i, col])
        return remote(src, dst, g_ssem, g_rsem.at[i, col], to_ring(i, (s1 * 2 + jd + col) % 4, second, cd, zd))

    def f_step(i, col):
        for n in range(len(pieces(i))):
            b_copy(i, col, n).wait_recv()
        value = bown_v[i, col] + brecv_v[i, col].astype(F32)
        tiles = [value[:, 128 * n : 128 * (n + 1)] for n in range(5)]
        lower = lax.broadcasted_iota(jnp.int32, (32, 128), 0) % 8 >= 4
        for w in range(2):
            win, rest = tiles[2 * w : 2 * w + 3], (tiles[3:] if w == 0 else tiles[:2])
            shared = jnp.where(lower, rest[0], pltpu.roll(rest[1], 28, 0))
            upper = jnp.concatenate([win[0], win[1]], axis=1).reshape(4, 8, 256)
            under = jnp.concatenate([win[2], shared], axis=1).reshape(4, 8, 256)
            gsend_v[i, col, w] = jnp.concatenate([upper, under], axis=1).reshape(64, 256).astype(BF)
        for d in (7, 6, 5, 4, 3, 2, 1, 0):
            g_copy(i, col, d).start()

    def y_copy(i, col, d):
        return remote(
            ysend_v.at[i, col, d - 1], rows_v.at[y, i, col],
            y_ssem, y_rsem.at[i], dev(zl, (y + d) % 4, x, zh, c),
        )

    def y_step(i, col):
        landed(gath_v.at[i * 2 + col], g_rsem.at[i, col])
        packed = gath_v[i * 2 + col]
        upper = dot(order_v[0], packed).astype(BF)
        under = dot(order_v[1], packed).astype(BF)
        win = [upper[:32, :128], upper[:32, 128:], under[:32, :128]]
        rest = [under[:32, 128:], under[32:, 128:]]
        right = jnp.where(zl == 0, jnp.concatenate(win + rest, axis=1), jnp.concatenate(rest + win, axis=1))
        pick_copy = dot(jnp.concatenate([upper[32:], under[32:, :128]], axis=1), pick_v[...]).astype(BF)
        lefts = [pick_copy[:, 128 * n : 128 * (n + 1)] for n in range(4)]
        for d in (2, 1, 3, 0):
            to = (y + d) % 4
            left = jnp.where(to < 2, jnp.where(to == 0, lefts[0], lefts[1]), jnp.where(to == 2, lefts[2], lefts[3]))
            if d:
                ysend_v[i, col, d - 1, :, :natural] = right
                ysend_v[i, col, d - 1, :, natural:] = left
                y_copy(i, col, d).start()
            else:
                rows_v[y, i, col, :, :natural] = right
                rows_v[y, i, col, :, natural:] = left

    def out_step(i, last):
        landed(rows_v.at[pl.ds(0, 3), i], y_rsem.at[i])
        both = rows_v[:, i].reshape(256, natural + 128)
        left = both[:, natural:]
        parity = lax.broadcasted_iota(jnp.int32, left.shape, 0) % 2
        zero = jnp.zeros_like(left)
        left = jnp.concatenate([jnp.where(parity == t, left, zero) for t in range(2)], axis=1)
        total = acc_v[...] + lax.dot_general(
            left, both[:, :natural], (((0,), (0,)), ((), ())), preferred_element_type=F32
        )
        if last:
            for t in range(2):
                out_ref[:, t, :] = total[128 * t : 128 * t + 80]
        else:
            acc_v[...] = total

    def one_hots():
        to = lax.broadcasted_iota(jnp.int32, (64, 128), 0)
        at = lax.broadcasted_iota(jnp.int32, (64, 128), 1)
        source = (to % 32) // 4 * 16 + to % 4 + jnp.where(to < 32, 4, 0)
        for n in range(2):
            order_v[n] = jnp.where(at == source + 8 * n, 1.0, 0.0).astype(BF)
        at = lax.broadcasted_iota(jnp.int32, (384, 512), 0)
        to = lax.broadcasted_iota(jnp.int32, (384, 512), 1)
        source = (zl * 4 + to // 128) * 80 + to % 128 - zl * 256
        pick_v[...] = jnp.where((at == source) & (to % 128 < 80), 1.0, 0.0).astype(BF)
        acc_v[...] = jnp.zeros_like(acc_v)

    def drain_step():
        landed(pair_v.at[0, pl.ds(0, 7)], p_ssem.at[0])
        landed(pack_v.at[pl.ds(0, 3)], p_ssem.at[1])
        landed(half_v.at[pl.ds(0, 3)], h_ssem)
        landed(tsend_v, t_ssem)
        landed(asend_v, a_ssem)
        landed(bsend_v, b_ssem)
        landed(gath_v.at[pl.ds(0, 2 * ROUNDS - 1)], g_ssem)

    steps = {"t": t_step, "a": a_step, "b": b_step, "f": f_step, "y": y_step}
    for token in PLAN:
        name, i = token[0], int(token[1])
        if name == "h":
            half_step(i)
            half_send(i, FIRST if i in LATE else FIRST + SECOND)
        elif name == "s":
            half_send(i, SECOND)
        elif name == "o":
            out_step(i, token == PLAN[-1])
        elif name == "d":
            drain_step()
        elif name == "p":
            p_step()
        elif name == "w":
            w_step(i)
        elif name == "c":
            one_hots()
        elif name in "tab":
            for n in (int(token[2]),) if len(token) > 2 else range(len(pieces(i))):
                for col in range(2):
                    steps[name](i, col, n)
            if name == "t":
                for col in range(2):
                    t_own_step(i, col)
        else:
            for col in range(2):
                steps[name](i, col)

    landed(ysend_v, y_ssem)


def constants():
    k = np.arange(4 * SUB * 40)
    dev, fun, orb = k // (SUB * 40), (k // 40) % SUB, k % 40
    a = np.arange(80)
    spread = np.stack(
        [(dev[None] == 2 * jj + a[:, None] // 40) & (orb[None] == a[:, None] % 40) for jj in range(2)]
    )
    r = np.arange(256)
    mask = ((r[:, None] // 2) % SUB) == fun[None]
    return spread.astype(np.float32), mask.astype(np.float32)


def solution(mesh):
    spread, mask = constants()

    def local(df_blocks, fno_rotation, tile_pairs):
        aux_n, orbs, nv = df_blocks.shape
        nf = fno_rotation.shape[1]
        rows = aux_n * orbs // ROUNDS
        vm = pltpu.VMEM
        dma = pltpu.SemaphoreType.DMA
        return pl.pallas_call(
            kernel,
            name="tiles",
            out_shape=pltpu.VMEM((80, 2, nf), F32),
            in_specs=[
                pl.BlockSpec(memory_space=pl.ANY),
                pl.BlockSpec(memory_space=pl.ANY),
                pl.BlockSpec(memory_space=pltpu.SMEM),
                pl.BlockSpec(memory_space=pl.ANY),
                pl.BlockSpec(memory_space=pl.ANY),
            ],
            out_specs=pl.BlockSpec(memory_space=pltpu.VMEM),
            scratch_shapes=[
                vm((2, 80, 4 * SUB * 40), BF),
                vm((256, 4 * SUB * 40), BF),
                vm((ROUNDS, rows, nv), BF),
                vm((nv, nf), BF),
                vm((ROUNDS, rows, nf), BF),
                vm((ROUNDS, 2, rows // 2, nf), BF),
                vm((4, 8, 8, 128), jnp.int32),
                vm((4, 8, 128), jnp.int32),
                vm((256, nf), BF),
                vm((4, 256, 4 * SUB * 40), BF),
                vm((ROUNDS, 2, 128, nf), BF),
                vm((ROUNDS, 2, 128, nf), F32),
                vm((ROUNDS, 2, 128, nf), BF),
                vm((ROUNDS, 2, 64, nf), BF),
                vm((ROUNDS, 2, 64, nf), F32),
                vm((ROUNDS, 2, 64, nf), BF),
                vm((ROUNDS, 2, 32, nf), BF),
                vm((ROUNDS, 2, 32, nf), F32),
                vm((ROUNDS, 2, 32, nf), BF),
                vm((ROUNDS, 2, 2, 64, 256), BF),
                vm((ROUNDS * 2, 128, 256), BF),
                vm((2, 64, 128), BF),
                vm((384, 512), BF),
                vm((4, ROUNDS, 2, 32, nf + 128), BF),
                vm((ROUNDS, 2, 3, 32, nf + 128), BF),
                vm((256, nf), F32),
                dma((2,)),
                dma((ROUNDS,)),
                dma(()),
                dma((2,)), dma((2,)),
                dma(()), dma((ROUNDS, 2)),
                dma(()), dma((ROUNDS, 2, 3)),
                dma(()), dma((ROUNDS, 2, 3)),
                dma(()), dma((ROUNDS, 2, 3)),
                dma(()), dma((ROUNDS, 2)),
                dma(()), dma((ROUNDS,)),
            ],
            compiler_params=pltpu.CompilerParams(
                collective_id=0, has_side_effects=True, vmem_limit_bytes=59392 * 2**10
            ),
        )(
            df_blocks.reshape(aux_n * orbs, nv),
            fno_rotation,
            tile_pairs,
            jnp.asarray(spread, BF),
            jnp.asarray(mask, BF),
        )

    placed = (P("aux", "virt", None), P(), P("virt", None))
    return jax.shard_map(local, mesh=mesh, in_specs=placed, out_specs=P("aux", "virt", None), check_vma=False)
```
